512 devices in a mesh: exc: 16 (over z_lo, y), unk: 32 (over z_hi, x, core).
Axes of the slice: x: 4, y: 8, z: 8 (z_hi: 4, z_lo: 2; z = z_hi * 2 + z_lo), core: 2. Of those that a mesh axis runs over, the one named last changes fastest.
Arguments:
- responses: bfloat16 [2, 4, 1440, 16384], P(None, None, 'exc', 'unk'), may hold values from -6 to 6
- eigvecs: bfloat16 [1440, 11520], P('exc'), may hold values from -0.15625 to 0.15625
Outputs:
- gram: float32 [2, 4, 1440, 1440], P(None, None, 'exc', 'unk')
- basis: bfloat16 [2, 4, 1440, 16384], P(None, None, 'exc', 'unk')
The draws below stay inside these ranges and needn't reach their ends.
All inputs are finite; a program needn't handle non-finite values.
Results may differ from the reference program's by a relative error of at most 0.0005.
Values may be sent and summed in bfloat16 or wider, within the bound.
A program may use at most 128 MiB of HBM per device.

```python
import jax
import jax.numpy as jnp
from jax import lax

PLANE_WAVES = 1440
BASIS_PER_BLOCK = 1440
ROWS_DEV = 512
EXTENDED_BLOCKS = 4
UNKNOWNS = 16384
N_UNK = 32


def raised(drawn, stream_key, source, target, shards_of, factor):
    owner, partner = [(jnp.arange(drawn.shape[dim]) // (drawn.shape[dim] // shards_of)).reshape([-1 if axis == dim else 1 for axis in range(drawn.ndim)]) for dim in (source, target)]
    chosen = jax.random.permutation(stream_key, shards_of)[partner]
    strong = (owner == chosen) | (owner == (partner + shards_of // 2) % shards_of)
    return jnp.where(strong, factor * drawn, drawn)


def block_levels(own_key, shape, shards, least, largest):
    loudness = 1.0
    for position, blocks in shards:
        heights = jax.random.uniform(jax.random.fold_in(jax.random.fold_in(own_key, 6), position), (blocks,), jnp.float32, least / len(shards), largest / len(shards))
        loudness = loudness * jnp.repeat(jnp.exp(heights), shape[position] // blocks).reshape((-1,) + (1,) * (len(shape) - 1 - position))
    return loudness


def noise(rng, shape, spread, reach, cuts=(), kind=jnp.bfloat16):
    drawn = jax.random.normal(rng, shape, jnp.float32) * spread
    if len(cuts) > 0:
        drawn = block_levels(rng, shape, cuts, -0.22, 0.18) * drawn
    return jnp.clip(drawn, min=-reach, max=reach).astype(kind)


def heavy_noise(stream_key, shape, scale, reach, cuts, heavy, kind=jnp.bfloat16):
    result = scale * jax.random.normal(stream_key, shape, jnp.float32)
    if cuts:
        result = result * block_levels(stream_key, shape, cuts, -0.22, 0.18)
    return jnp.clip(raised(result, jax.random.fold_in(stream_key, 3), *heavy), -reach, reach).astype(kind)


def setup_inputs(seed: int = 0) -> dict:
    splits = jax.random.split(jax.random.key(seed), 3)
    return {
        "responses": heavy_noise(splits[0], (2, EXTENDED_BLOCKS, PLANE_WAVES, UNKNOWNS), 1.0, 6.0, ((2, 16), (3, 32)), (3, 2, 32, 2.75)),
        "eigvecs": noise(splits[1], (BASIS_PER_BLOCK, 2 * EXTENDED_BLOCKS * PLANE_WAVES), PLANE_WAVES ** -0.5, 0.15625, ((0, 16),)),
    }


def slab_partial(running, shard_rows):
    real_rows = shard_rows[0]
    imag_rows = shard_rows[1]
    real_real = jnp.dot(real_rows, real_rows.T, preferred_element_type=jnp.float32)
    imag_imag = jnp.dot(imag_rows, imag_rows.T, preferred_element_type=jnp.float32)
    real_imag = jnp.dot(real_rows, imag_rows.T, preferred_element_type=jnp.float32)
    imag_real = jnp.dot(imag_rows, real_rows.T, preferred_element_type=jnp.float32)
    partial_sum = jnp.stack([real_real + imag_imag, real_imag - imag_real]) / float(UNKNOWNS)
    return running + partial_sum, None


def block_gram(block_resp):
    slabs = block_resp.reshape(2, PLANE_WAVES, N_UNK, ROWS_DEV)
    slabs = jnp.transpose(slabs, (2, 0, 1, 3))
    running, _ = lax.scan(slab_partial, jnp.zeros((2, PLANE_WAVES, PLANE_WAVES), jnp.float32), slabs)
    return running


def block_basis(pair):
    block_resp, block_eig = pair
    real_rows = block_resp[0]
    imag_rows = block_resp[1]
    real_vec = block_eig[:, 0, :]
    imag_vec = block_eig[:, 1, :]
    real_part = jnp.dot(real_vec, real_rows, preferred_element_type=jnp.float32) - jnp.dot(imag_vec, imag_rows, preferred_element_type=jnp.float32)
    imag_part = jnp.dot(imag_vec, real_rows, preferred_element_type=jnp.float32) + jnp.dot(real_vec, imag_rows, preferred_element_type=jnp.float32)
    return jnp.stack([real_part, imag_part]).astype(jnp.bfloat16)


def reference(responses, eigvecs):
    by_block = jnp.moveaxis(responses, 1, 0)
    eigen_division = jnp.moveaxis(eigvecs.reshape(BASIS_PER_BLOCK, 2, EXTENDED_BLOCKS, PLANE_WAVES), 2, 0)
    gram = jnp.moveaxis(lax.map(block_gram, by_block), 0, 1)
    basis = jnp.moveaxis(lax.map(block_basis, (by_block, eigen_division)), 0, 1)
    return gram, basis
```

```python
import jax
import jax.numpy as jnp
from jax import lax
from jax.experimental import pallas as pl
from jax.experimental.pallas import tpu as pltpu
from jax.sharding import PartitionSpec as P

MESH = pl.DeviceIdType.MESH
ROWS, PAD, HALF = 90, 96, 256
BLOCKS, RING, GROUPS = 4, 8, 16
WAVES = ROWS * GROUPS
KDIM = PAD * GROUPS
F32 = jnp.float32


def mod(value, size):
    return lax.rem(value + 2 * size, size)


def device(x, y, zh, zl, c):
    return {"exc": zl * 8 + y, "unk": (zh * 4 + x) * 2 + c}


def pick(flag, one, other):
    return flag * one + (1 - flag) * other


def kernel(
    x_ref, e_ref, basis_ref, gram_ref,
    xs, staged, ee, bsend, bland, parts, core_in, x1_in, x2_in, zl_in, zh_in, zsum, done, fin_in,
    pair_s, pair_r, ring_s, ring_r, eig_s, eig_r, fwd_s, fwd_r, out_s, out_r,
    core_s, core_r, x1_s, x1_r, x2_s, x2_r, zl_s, zl_r, zh_s, zh_r, fin_s, fin_r,
):
    exc, unk = lax.axis_index("exc"), lax.axis_index("unk")
    zl, y = exc // 8, exc % 8
    zh, x, c = unk // 8, (unk // 2) % 4, unk % 2
    other = 1 - zl
    up, down = device(x, mod(y + 1, 8), zh, zl, c), device(x, mod(y - 1, 8), zh, zl, c)
    pair = device(x, y, zh, other, c)
    znext = device(x, y, mod(zh + zl, 4), other, c)
    zprev = device(x, y, mod(zh - other, 4), other, c)
    sibling = device(x, y, zh, zl, 1 - c)
    xup, xdown = device(mod(x + 1, 4), y, zh, zl, c), device(mod(x - 1, 4), y, zh, zl, c)
    zothers = [device(x, y, mod(zh + k, 4), zl, c) for k in (1, 2, 3)]
    kap = mod(x - y, 4)
    jy = mod(y + kap - 4 * (kap // 3), 8)
    plus = jnp.where((kap == 0) | (kap == 3), 1, 0)
    ioff = pick(plus, kap // 3 + c, -(kap // 2 + c))
    iy = mod(y + ioff, 8)
    dest_zh = zl * 2 + jy // 4
    dests = [(zi, cc) for zi in (0, 1) for cc in (0, 1)]
    is_self = [(iy == y) & (dest_zh == zh) & (zl == zi) & (c == cc) for zi, cc in dests]
    my_j = (zh % 2) * 4 + x
    delta = mod(my_j - y, 8)
    src_y = jnp.where(
        delta == 0, my_j,
        jnp.where(delta == 7, my_j,
        jnp.where(delta <= 2, mod(my_j - 1, 8),
        jnp.where(delta <= 4, mod(my_j - 2, 8), mod(my_j + 1, 8)))))
    src_c = jnp.where((delta == 7) | (delta == 2) | (delta == 4) | (delta == 5), 1, 0)
    src_zl = zh // 2
    from_self = [(src_y == y) & (src_zl == zl) & (src_c == c) & (zh == g) for g in range(4)]

    def remote(src, dst, send, recv, to):
        return pltpu.make_async_remote_copy(
            src_ref=src, dst_ref=dst, send_sem=send, recv_sem=recv, device_id=to, device_id_type=MESH
        )

    barrier = pltpu.get_barrier_semaphore()

    def greet(to):
        pl.semaphore_signal(barrier, inc=1, device_id=to, device_id_type=MESH)

    around = [up, down, znext, zprev, sibling, xup, xdown] + zothers
    for to in around:
        greet(to)
    for g in range(4):
        pl.when(jnp.logical_not(from_self[g]))(lambda g=g: greet(device(x, src_y, g, src_zl, src_c)))
    selves = sum(jnp.where(f, 1, 0) for f in is_self)
    pl.semaphore_wait(barrier, len(around) + 4 - selves)

    zero = jnp.zeros((16, 2 * HALF), jnp.bfloat16)

    def pair_copy(b):
        return remote(staged.at[b], xs.at[b, zl, y], pair_s.at[b], pair_r.at[b], pair)

    def pair_recv(b):
        return remote(staged.at[b], xs.at[b, other, y], pair_s.at[b], pair_r.at[b], pair)

    for b in range(BLOCKS):
        p, q = x_ref[0, b], x_ref[1, b]
        low = jnp.concatenate([p[:, :HALF], q[:, :HALF]], axis=1)
        high = jnp.concatenate([p[:, HALF:], q[:, HALF:]], axis=1)
        first = jnp.full(low.shape, zl, jnp.int32) == 0
        staged[b, 80:96, :] = zero
        staged[b, 0:ROWS, :] = jnp.where(first, high, low)
        pair_copy(b).start()
        xs[b, zl, y, 80:96, :] = zero
        xs[b, zl, y, 0:ROWS, :] = jnp.where(first, low, high)

    def ring(way, b, d):
        src = mod(y - (d - 1), 8) if way == 0 else mod(y + (d - 1), 8)
        ref = xs.at[b, :, src] if d < 4 else xs.at[b, way, src]
        return remote(ref, ref, ring_s.at[way, b, d - 1], ring_r.at[way, b, d - 1], (up, down)[way])

    def ring_recv(way, b, d):
        src = mod(y - d, 8) if way == 0 else mod(y + d, 8)
        ref = xs.at[b, :, src] if d < 4 else xs.at[b, way, src]
        return remote(ref, ref, ring_s.at[way, b, d - 1], ring_r.at[way, b, d - 1], (up, down)[way])

    def pack_eig(b):
        for part in range(2):
            ee[b, 0, part] = jnp.zeros((PAD, KDIM), jnp.bfloat16)
            base = (part * BLOCKS + b) * WAVES
            for i in range(GROUPS):
                ee[b, 0, part, 0:ROWS, i * PAD : i * PAD + ROWS] = e_ref[:, base + i * ROWS : base + (i + 1) * ROWS]

    def eig_copy(k):
        b = 2 * k + c
        return remote(ee.at[b, 0], ee.at[b, 1], eig_s.at[k], eig_r.at[k], (znext, zprev)[k])

    def eig_recv(k):
        b = 2 * k + c
        return remote(ee.at[b, 0], ee.at[b, 1], eig_s.at[k], eig_r.at[k], (znext, zprev)[k])

    def eig_forward(k):
        b = 2 * k + c
        return remote(ee.at[b, 1], ee.at[b, 1], fwd_s.at[k], fwd_r.at[k], sibling)

    def eig_forward_recv(k):
        b = 2 * k + 1 - c
        return remote(ee.at[b, 1], ee.at[b, 1], fwd_s.at[k], fwd_r.at[k], sibling)

    def gram_partial(b):
        def one(t, _):
            k, s = t // 2, t % 2
            joff = k - 4 * (k // 3)
            pos = jnp.where((k == 0) | (k == 3), 1, 0)
            off = pick(pos, k // 3 + s, -(k // 2 + s))
            rows = xs[b, :, mod(y + joff, 8)].reshape(2 * PAD, 2 * HALF)
            cols = []
            for zi in range(2):
                v = xs[b, zi, mod(y + off, 8)]
                cols += [v, jnp.concatenate([-v[:, HALF:], v[:, :HALF]], axis=1)]
            right = jnp.concatenate(cols, axis=0)
            parts[b, s, k] = lax.dot_general(rows, right, (((1,), (1,)), ((), ())), preferred_element_type=F32)
            return 0

        lax.fori_loop(0, 8, one, 0)
        core_copy(b).start()

    def core_copy(b):
        return remote(parts.at[b, 1 - c], core_in.at[b], core_s.at[b], core_r.at[b], sibling)

    k_up, k_down, k_far = mod(x + 1 - y, 4), mod(x - 1 - y, 4), mod(x + 2 - y, 4)

    def x1_copy(b, way):
        return remote(
            parts.at[b, c, k_far, way * PAD : (way + 1) * PAD], x1_in.at[b, way],
            x1_s.at[b, way], x1_r.at[b, way], (xup, xdown)[way],
        )

    def x2_copy(b, way):
        return remote(
            parts.at[b, c, (k_up, k_down)[way]], x2_in.at[b, way], x2_s.at[b, way], x2_r.at[b, way], (xup, xdown)[way]
        )

    def zl_copy(b):
        rows = pl.ds(pl.multiple_of(other * PAD, PAD), PAD)
        return remote(parts.at[b, c, kap, rows], zl_in.at[b], zl_s.at[b], zl_r.at[b], pair)

    def zh_copy(b, k):
        rows = pl.ds(pl.multiple_of(mod(zh + k, 4) * 24, 8), 24)
        return remote(zsum.at[b, rows], zh_in.at[b, k - 1], zh_s.at[b, k - 1], zh_r.at[b, k - 1], zothers[k - 1])

    def stage_core(b):
        core_copy(b).wait_recv()

        def add(k, _):
            parts[b, c, k] += core_in[b, k]
            return 0

        lax.fori_loop(0, 4, add, 0)
        x1_copy(b, 0).start()
        x1_copy(b, 1).start()

    def stage_x1(b):
        for way, k in ((0, k_up), (1, k_down)):
            x1_copy(b, way).wait_recv()
            parts[b, c, k, way * PAD : (way + 1) * PAD] += x1_in[b, way]
            x2_copy(b, way).start()

    def stage_x2(b):
        x2_copy(b, 0).wait_recv()
        x2_copy(b, 1).wait_recv()
        parts[b, c, kap] += x2_in[b, 0] + x2_in[b, 1]
        zl_copy(b).start()

    def stage_zl(b):
        zl_copy(b).wait_recv()
        rows = pl.ds(pl.multiple_of(zl * PAD, PAD), PAD)
        zsum[b] = parts[b, c, kap, rows] + zl_in[b]
        for k in (1, 2, 3):
            zh_copy(b, k).start()

    def fin_rows(g):
        return pl.ds(pl.multiple_of(g * 24, 8), 24)

    def fin_copy(b, n):
        zi, cc = dests[n]
        return remote(
            done.at[b, :, zi * 128 : zi * 128 + 256], fin_in.at[b, fin_rows(zh)],
            fin_s.at[b, n], fin_r.at[b, zh], device(x, iy, dest_zh, zi, cc),
        )

    def fin_local(b, n):
        zi, cc = dests[n]
        return pltpu.make_async_copy(
            done.at[b, :, zi * 128 : zi * 128 + 256], fin_in.at[b, fin_rows(zh)], fin_r.at[b, zh]
        )

    def stage_zh(b):
        for k in (1, 2, 3):
            zh_copy(b, k).wait_recv()
        done[b] = zsum[b, fin_rows(zh)] + zh_in[b, 0] + zh_in[b, 1] + zh_in[b, 2]
        for n in range(4):
            pl.when(is_self[n])(lambda n=n: fin_local(b, n).start())
            pl.when(jnp.logical_not(is_self[n]))(lambda n=n: fin_copy(b, n).start())

    def stage_fin(b):
        for g in range(4):
            remote(
                done.at[b, :, 0:256], fin_in.at[b, fin_rows(g)], fin_s.at[b, 0], fin_r.at[b, g], sibling
            ).wait_recv()
        gram_ref[b] = fin_in[b] * (1.0 / 16384.0)

    def out_copy(b):
        return remote(bsend.at[b], bland.at[b], out_s.at[b], out_r.at[b], pair)

    mine = pl.ds(pl.multiple_of(zl * HALF, HALF), HALF)
    theirs = pl.ds(pl.multiple_of(other * HALF, HALF), HALF)

    def basis(b):
        waves = xs[b].reshape(KDIM, 2 * HALF)
        for slot in (1, 0):
            rows = ee[b, slot].reshape(2 * PAD, KDIM)
            prod = jnp.dot(rows, waves, preferred_element_type=F32)
            re = (prod[:PAD, :HALF] - prod[PAD:, HALF:]).astype(jnp.bfloat16)
            im = (prod[PAD:, :HALF] + prod[:PAD, HALF:]).astype(jnp.bfloat16)
            if slot == 1:
                bsend[b, 0] = re
                bsend[b, 1] = im
                out_copy(b).start()
            else:
                basis_ref[0, b, :, mine] = re
                basis_ref[1, b, :, mine] = im

    def basis_land(b):
        out_copy(b).wait_recv()
        for part in range(2):
            basis_ref[part, b, :, theirs] = bland[b, part]

    for b in (0, 1, 2, 3):
        pair_recv(b).wait_recv()
        for way in (0, 1):
            ring(way, b, 1).start()
    pack_eig(0)
    pack_eig(1)

    def eig_a():
        eig_copy(0).start()

    def eig_b():
        pack_eig(2)

    def eig_c():
        pack_eig(3)
        eig_copy(1).start()

    def eig_d(k):
        eig_recv(k).wait_recv()
        eig_forward(k).start()

    todo = {
        0: [eig_a, eig_b],
        1: [eig_c],
        2: [lambda: gram_partial(0)],
        3: [lambda: stage_core(0), lambda: gram_partial(1)],
        4: [lambda: stage_core(1)],
        5: [lambda: stage_x1(0)],
        6: [lambda: stage_x1(1), lambda: gram_partial(2)],
        7: [lambda: stage_core(2), lambda: gram_partial(3)],
        8: [lambda: stage_x2(0), lambda: stage_core(3), lambda: eig_d(0)],
        9: [lambda: stage_x1(2), lambda: stage_zl(0), lambda: stage_x2(1)],
        10: [lambda: stage_x1(3), lambda: stage_zl(1), lambda: stage_zh(0), lambda: eig_d(1)],
        11: [lambda: stage_x2(2), lambda: stage_zh(1)],
        12: [lambda: stage_fin(0), lambda: stage_zl(2), lambda: stage_x2(3)],
        13: [lambda: stage_fin(1), lambda: stage_zl(3)],
        14: [lambda: stage_zh(2)],
        15: [lambda: stage_zh(3)],
    }
    order = [(0, 1), (1, 1), (0, 2), (1, 2), (2, 1), (3, 1), (2, 2), (3, 2)]
    order += [(b, d) for d in (3, 4) for b in range(BLOCKS)]
    for slot, (b, d) in enumerate(order):
        for way in (0, 1):
            ring_recv(way, b, d).wait_recv()
            if d < 4:
                ring(way, b, d + 1).start()
        if slot == 12:
            eig_forward_recv(0).wait_recv()
            eig_forward_recv(1).wait_recv()
        if d == 4:
            basis(b)
        for act in todo.get(slot, ()):
            act()
    stage_fin(2)
    stage_fin(3)
    for b in range(BLOCKS):
        basis_land(b)

    for b in range(BLOCKS):
        pair_copy(b).wait_send()
        for d in (1, 2, 3, 4):
            for way in (0, 1):
                ring(way, b, d).wait_send()
        out_copy(b).wait_send()
        core_copy(b).wait_send()
        for way in (0, 1):
            x1_copy(b, way).wait_send()
            x2_copy(b, way).wait_send()
        zl_copy(b).wait_send()
        for k in (1, 2, 3):
            zh_copy(b, k).wait_send()
        for n in range(4):
            pl.when(jnp.logical_not(is_self[n]))(lambda n=n, b=b: fin_copy(b, n).wait_send())
    for k in (0, 1):
        eig_copy(k).wait_send()
        eig_forward(k).wait_send()


def local(responses, eigvecs):
    dma = pltpu.SemaphoreType.DMA
    bf, vm = jnp.bfloat16, pltpu.VMEM
    basis, gram = pl.pallas_call(
        kernel,
        out_shape=(
            jax.ShapeDtypeStruct((2, BLOCKS, PAD, 2 * HALF), bf),
            jax.ShapeDtypeStruct((BLOCKS, PAD, 256), F32),
        ),
        in_specs=[pl.BlockSpec(memory_space=vm)] * 2,
        out_specs=(pl.BlockSpec(memory_space=vm),) * 2,
        scratch_shapes=[
            vm((BLOCKS, 2, RING, PAD, 2 * HALF), bf),
            vm((BLOCKS, PAD, 2 * HALF), bf),
            vm((BLOCKS, 2, 2, PAD, KDIM), bf),
            vm((BLOCKS, 2, PAD, HALF), bf),
            vm((BLOCKS, 2, PAD, HALF), bf),
            vm((BLOCKS, 2, 4, 2 * PAD, 4 * PAD), F32),
            vm((BLOCKS, 4, 2 * PAD, 4 * PAD), F32),
            vm((BLOCKS, 2, PAD, 4 * PAD), F32),
            vm((BLOCKS, 2, 2 * PAD, 4 * PAD), F32),
            vm((BLOCKS, PAD, 4 * PAD), F32),
            vm((BLOCKS, 3, 24, 4 * PAD), F32),
            vm((BLOCKS, PAD, 4 * PAD), F32),
            vm((BLOCKS, 24, 4 * PAD), F32),
            vm((BLOCKS, PAD, 256), F32),
            dma((4,)), dma((4,)), dma((2, 4, 4)), dma((2, 4, 4)),
            dma((2,)), dma((2,)), dma((2,)), dma((2,)), dma((4,)), dma((4,)),
            dma((4,)), dma((4,)), dma((4, 2)), dma((4, 2)), dma((4, 2)), dma((4, 2)),
            dma((4,)), dma((4,)), dma((4, 3)), dma((4, 3)), dma((4, 4)), dma((4, 4)),
        ],
        compiler_params=pltpu.CompilerParams(
            collective_id=0, has_side_effects=True, vmem_limit_bytes=60 * 2**20
        ),
    )(responses, eigvecs)
    zl = lax.axis_index("exc") // 8
    c = lax.axis_index("unk") % 2
    mine = lax.dynamic_slice(gram, (0, c * 45, zl * 64), (BLOCKS, 45, 2 * PAD))
    mine = mine.reshape(BLOCKS, 45, 2, PAD)[..., :ROWS]
    return jnp.transpose(mine, (2, 0, 3, 1)), basis[:, :, :ROWS]


def solution(mesh):
    specs = P(None, None, "exc", "unk")
    return jax.shard_map(local, mesh=mesh, in_specs=(specs, P("exc", None)), out_specs=(specs, specs), check_vma=False)
```

```python
import jax
import jax.numpy as jnp
from jax import lax
from jax.experimental import pallas as pl
from jax.experimental.pallas import tpu as pltpu
from jax.sharding import PartitionSpec as P

MESH = pl.DeviceIdType.MESH
ROWS, PAD, HALF = 90, 96, 256
BLOCKS, RING, GROUPS = 4, 8, 16
WAVES = ROWS * GROUPS
KDIM = PAD * GROUPS
ZH_SLOT = 1
CUT = 56
F32 = jnp.float32


def mod(value, size):
    return lax.rem(value + 2 * size, size)


def device(x, y, zh, zl, c):
    return {"exc": zl * 8 + y, "unk": (zh * 4 + x) * 2 + c}


def row_of(k):
    return k - 4 * (k // 3)


def col_of(k, s):
    plus = jnp.where((k == 0) | (k == 3), 1, 0)
    return plus * (k // 3 + s) - (1 - plus) * (k // 2 + s)


def kernel(
    x_ref, e_ref, basis_ref, gram_ref,
    xs, staged, window, ee, bsend, bland, parts, core_in, zl_in, zsum, zh_in, done, fin_in,
    scat_s, scat_r, near_s, near_r, ring_s, ring_r, win_s, eig_s, eig_r, fwd_s, fwd_r, out_s, out_r,
    core_s, core_r, zl_s, zl_r, zh_s, zh_r, fin_s, fin_r, above,
):
    exc, unk = lax.axis_index("exc"), lax.axis_index("unk")
    zl, y = exc // 8, exc % 8
    zh, x, c = unk // 8, (unk // 2) % 4, unk % 2
    other = 1 - zl
    up, down = device(x, mod(y + 1, 8), zh, zl, c), device(x, mod(y - 1, 8), zh, zl, c)
    pair = device(x, y, zh, other, c)
    sibling = device(x, y, zh, zl, 1 - c)
    pool = [(o, t) for o in (0, 1, 3, 2) for t in (0, 1) if (o, t) != (0, 0)]

    def pooled(o, t):
        return device(mod(x + o, 4), y, zh, (zl, other)[t], c)

    jy, iy = mod(y + row_of(zh), 8), mod(y + col_of(zh, c), 8)
    dests = [(zi, cc) for zi in (0, 1) for cc in (0, 1)]
    dest_x, dest_zh = jy % 4, zl * 2 + jy // 4
    same = (dest_x == x) & (iy == y) & (dest_zh == zh)
    is_self = [same & (zl == zi) & (c == cc) for zi, cc in dests]
    def remote(src, dst, send, recv, to):
        return pltpu.make_async_remote_copy(
            src_ref=src, dst_ref=dst, send_sem=send, recv_sem=recv, device_id=to, device_id_type=MESH
        )

    def win_copy(part):
        first = pl.multiple_of((part * 4 + x) * 1408 + part * 128, 128)
        return pltpu.make_async_copy(e_ref.at[:, pl.ds(first, KDIM)], window.at[part], win_s.at[part])

    win_copy(0).start()
    win_copy(1).start()

    barrier = pltpu.get_barrier_semaphore()

    def greet(to):
        pl.semaphore_signal(barrier, inc=1, device_id=to, device_id_type=MESH)

    around = [up, down, sibling] + [pooled(o, t) for o, t in pool]
    for to in around:
        greet(to)
    for k in (1, 2, 3):
        pl.when(zh < k)(lambda k=k: greet(device(x, y, k, zl, c)))
    pl.semaphore_wait(barrier, len(around) + zh)
    for k in (0, 1, 2):

        @pl.when(zh > k)
        def _():
            pl.semaphore_signal(above, inc=1, device_id=device(x, y, k, zl, c), device_id_type=MESH)

    zero = jnp.zeros((PAD - 80, 2 * HALF), jnp.bfloat16)

    def scat_copy(o, t):
        return remote(staged.at[mod(x + o, 4), t], xs.at[x, zl, y], scat_s.at[o, t], scat_r.at[x, zl], pooled(o, t))

    def scat_recv(o, t):
        q, z = mod(x + o, 4), (zl, other)[t]
        return remote(staged.at[q, t], xs.at[q, z, y], scat_s.at[o, t], scat_r.at[q, z], pooled(o, t))

    def near(way, o, t):
        q, z = mod(x + o, 4), (zl, other)[t]
        ref = xs.at[q, z, y]
        return remote(ref, ref, near_s.at[way, o, t], near_r.at[way, q, z], (up, down)[way])

    def near_recv(way, o, z):
        q = mod(x + o, 4)
        ref = xs.at[q, z, mod(y - 1, 8) if way == 0 else mod(y + 1, 8)]
        return remote(ref, ref, near_s.at[way, o, z], near_r.at[way, q, z], (up, down)[way])

    def ring_ref(way, o, d, hop):
        src = mod(y - hop, 8) if way == 0 else mod(y + hop, 8)
        q = mod(x + o, 4)
        return xs.at[q, :, src] if d < 4 else xs.at[q, way, src]

    def ring(way, o, d):
        ref = ring_ref(way, o, d, d - 1)
        return remote(ref, ref, ring_s.at[way, o, d - 2], ring_r.at[way, o, d - 2], (up, down)[way])

    def ring_recv(way, o, d):
        ref = ring_ref(way, o, d, d)
        return remote(ref, ref, ring_s.at[way, o, d - 2], ring_r.at[way, o, d - 2], (up, down)[way])

    for o in (0, 1, 3, 2):
        b = mod(x + o, 4)
        p, q = x_ref[0, b], x_ref[1, b]
        low = jnp.concatenate([p[:, :HALF], q[:, :HALF]], axis=1)
        high = jnp.concatenate([p[:, HALF:], q[:, HALF:]], axis=1)
        first = jnp.full(low.shape, zl, jnp.int32) == 0
        staged[b, 1, 80:96, :] = zero
        staged[b, 1, 0:ROWS, :] = jnp.where(first, high, low)
        scat_copy(o, 1).start()
        if o == 0:
            xs[b, zl, y, 80:96, :] = zero
            xs[b, zl, y, 0:ROWS, :] = jnp.where(first, low, high)
            near(0, 0, 0).start()
            near(1, 0, 0).start()
        else:
            staged[b, 0, 80:96, :] = zero
            staged[b, 0, 0:ROWS, :] = jnp.where(first, low, high)
            scat_copy(o, 0).start()

    def pack_eig():
        win_copy(0).wait()
        win_copy(1).wait()
        for part in range(2):
            ee[0, part] = jnp.zeros((PAD, KDIM), jnp.bfloat16)
        for at in range(4):

            @pl.when(x == at)
            def _():
                for part in range(2):
                    for i in range(GROUPS):
                        first = at * 32 + i * ROWS
                        ee[0, part, 0:ROWS, i * PAD : i * PAD + ROWS] = window[part, :, first : first + ROWS]

    def eig_copy():
        return remote(ee.at[0, c], ee.at[1, c], eig_s, eig_r, pair)

    def eig_forward():
        return remote(ee.at[1, c], ee.at[1, c], fwd_s, fwd_r, sibling)

    def eig_forward_recv():
        return remote(ee.at[1, 1 - c], ee.at[1, 1 - c], fwd_s, fwd_r, sibling)

    def gram_partial(n, o):
        q = mod(x + o, 4)

        def one(t, _):
            k, s = 2 * n + t // 2, t % 2
            rows = xs[q, :, mod(y + row_of(k), 8)].reshape(2 * PAD, 2 * HALF)
            cols = []
            for zi in range(2):
                v = xs[q, zi, mod(y + col_of(k, s), 8)]
                cols += [v, jnp.concatenate([-v[:, HALF:], v[:, :HALF]], axis=1)]
            right = jnp.concatenate(cols, axis=0)
            prod = lax.dot_general(rows, right, (((1,), (1,)), ((), ())), preferred_element_type=F32)
            parts[n, s, t // 2] += prod
            return 0

        lax.fori_loop(0, 4, one, 0)

    def core_copy(n):
        return remote(parts.at[n, 1 - c], core_in.at[n], core_s.at[n], core_r.at[n], sibling)

    def zl_copy(n):
        rows = pl.ds(pl.multiple_of(other * PAD, PAD), PAD)
        return remote(parts.at[n, c, :, rows], zl_in.at[n], zl_s.at[n], zl_r.at[n], pair)

    def zh_copy(k):
        slot = mod(zh - k, 4) - 1
        return remote(zsum.at[k], zh_in.at[slot], zh_s.at[k], zh_r.at[slot], device(x, y, k, zl, c))

    def zh_recv(slot):
        return remote(zsum.at[0], zh_in.at[slot], zh_s.at[0], zh_r.at[slot], sibling)

    def stage_core(n):
        core_copy(n).wait_recv()
        for k in range(2):
            parts[n, c, k] += core_in[n, k]
        zl_copy(n).start()

    def stage_zl(n):
        zl_copy(n).wait_recv()
        rows = pl.ds(pl.multiple_of(zl * PAD, PAD), PAD)
        for k in range(2):
            zsum[2 * n + k] = parts[n, c, k, rows] + zl_in[n, k]
            pl.when(zh != 2 * n + k)(lambda k=k: zh_copy(2 * n + k).start())

    def fin_refs(n):
        zi, cc = dests[n]
        return done.at[40 * cc : 40 * cc + CUT, zi * 128 : zi * 128 + 256], fin_in.at[x]

    def fin_copy(n):
        zi, cc = dests[n]
        src, dst = fin_refs(n)
        return remote(src, dst, fin_s.at[n], fin_r.at[x], device(dest_x, iy, dest_zh, zi, cc))

    def stage_zh():
        for slot in range(3):
            zh_recv(slot).wait_recv()
        done[...] = zsum[zh] + zh_in[0] + zh_in[1] + zh_in[2]
        for n in range(4):
            pl.when(is_self[n])(lambda n=n: pltpu.make_async_copy(*fin_refs(n), fin_r.at[x]).start())
            pl.when(jnp.logical_not(is_self[n]))(lambda n=n: fin_copy(n).start())

    def stage_fin():
        for b in range(BLOCKS):
            remote(done.at[0:CUT, 0:256], fin_in.at[b], fin_s.at[0], fin_r.at[b], sibling).wait_recv()
            gram_ref[b] = fin_in[b] * (1.0 / 16384.0)

    mine = pl.ds(pl.multiple_of(zl * HALF, HALF), HALF)
    theirs = pl.ds(pl.multiple_of(other * HALF, HALF), HALF)

    def out_copy(o, t):
        to = device(mod(x + o, 4), y, zh, zl + t * (other - zl), c)
        return remote(bsend.at[o, t], bland.at[x, zl], out_s.at[o, t], out_r.at[x, zl], to)

    def out_recv(o, t):
        b, half = mod(x + o, 4), (zl, other)[t]
        return remote(bsend.at[o, t], bland.at[b, half], out_s.at[o, t], out_r.at[b, half], pooled(o, t))

    def basis(o):
        q = mod(x + o, 4)

        def rows_of(n, _):
            t = 1 - n
            prod = jnp.dot(ee[t].reshape(2 * PAD, KDIM), xs[q].reshape(KDIM, 2 * HALF), preferred_element_type=F32)
            bsend[o, t, 0] = (prod[:PAD, :HALF] - prod[PAD:, HALF:]).astype(jnp.bfloat16)
            bsend[o, t, 1] = (prod[PAD:, :HALF] + prod[:PAD, HALF:]).astype(jnp.bfloat16)
            own = (o == 0) & (t == 0)

            @pl.when(own)
            def _():
                basis_ref[0, x, :, mine] = bsend[0, 0, 0]
                basis_ref[1, x, :, mine] = bsend[0, 0, 1]

            pl.when(jnp.logical_not(own))(lambda: out_copy(o, t).start())
            return 0

        lax.fori_loop(0, 2, rows_of, 0)

    def basis_land(o, t):
        out_recv(o, t).wait_recv()
        b, half = mod(x + o, 4), (zl, other)[t]
        for part in range(2):
            basis_ref[part, b, :, (mine, theirs)[t]] = bland[b, half, part]

    for o in (0, 3, 1, 2):
        for t in (0, 1):
            if (o, t) != (0, 0):
                scat_recv(o, t).wait_recv()
                near(0, o, t).start()
                near(1, o, t).start()
    pack_eig()
    eig_copy().start()
    parts[...] = jnp.zeros(parts.shape, F32)

    def hop_one(i, _):
        o = jnp.where(i == 0, 0, jnp.where(i == 1, 3, i - 1))
        for way in (0, 1):
            near_recv(way, o, 0).wait_recv()
            near_recv(way, o, 1).wait_recv()
            ring(way, o, 2).start()
        gram_partial(0, o)
        return 0

    def hop_two(i, _):
        o = jnp.where(i == 0, 0, jnp.where(i == 1, 3, i - 1))
        for way in (0, 1):
            ring_recv(way, o, 2).wait_recv()
            ring(way, o, 3).start()
        gram_partial(1, o)
        pl.when(i == 0)(lambda: stage_core(0))
        return 0

    def hop_three(i, _):
        o = jnp.where(i == 0, 0, jnp.where(i == 1, 3, i - 1))
        for way in (0, 1):
            ring_recv(way, o, 3).wait_recv()
            ring(way, o, 4).start()

        @pl.when(i == 0)
        def _():
            stage_core(1)
            eig_copy().wait_recv()
            eig_forward().start()

        pl.when(i == 2)(lambda: stage_zl(1))
        return 0

    def hop_four(i, _):
        o = jnp.where(i == 0, 3, jnp.where(i == 3, 0, i))
        for way in (0, 1):
            ring_recv(way, o, 4).wait_recv()
        basis(o)
        pl.when(i == ZH_SLOT)(stage_zh)
        return 0

    lax.fori_loop(0, 4, hop_one, 0)
    core_copy(0).start()
    lax.fori_loop(0, 4, hop_two, 0)
    core_copy(1).start()
    pl.when(zh < 3)(lambda: pl.semaphore_wait(above, 3 - zh))
    stage_zl(0)
    lax.fori_loop(0, 4, hop_three, 0)
    eig_forward_recv().wait_recv()
    lax.fori_loop(0, 4, hop_four, 0)
    for o in (1, 3, 2):
        for t in (0, 1):
            basis_land(o, t)
    stage_fin()
    basis_land(0, 1)

    for o, t in pool:
        scat_copy(o, t).wait_send()
        out_copy(o, t).wait_send()
    for way in (0, 1):
        for o in range(4):
            near(way, o, 0).wait_send()
            near(way, o, 1).wait_send()
            for d in (2, 3, 4):
                ring(way, o, d).wait_send()
    eig_copy().wait_send()
    eig_forward().wait_send()
    for n in range(2):
        core_copy(n).wait_send()
        zl_copy(n).wait_send()
    for k in range(4):
        pl.when(zh != k)(lambda k=k: zh_copy(k).wait_send())
        pl.when(jnp.logical_not(is_self[k]))(lambda k=k: fin_copy(k).wait_send())


def local(responses, eigvecs):
    dma = pltpu.SemaphoreType.DMA
    bf, vm = jnp.bfloat16, pltpu.VMEM
    basis, gram = pl.pallas_call(
        kernel,
        out_shape=(
            jax.ShapeDtypeStruct((2, BLOCKS, PAD, 2 * HALF), bf),
            jax.ShapeDtypeStruct((BLOCKS, CUT, 256), F32),
        ),
        in_specs=[pl.BlockSpec(memory_space=vm), pl.BlockSpec(memory_space=pl.ANY)],
        out_specs=(pl.BlockSpec(memory_space=vm),) * 2,
        scratch_shapes=[
            vm((4, 2, RING, PAD, 2 * HALF), bf),
            vm((4, 2, PAD, 2 * HALF), bf),
            vm((2, ROWS, KDIM), bf),
            vm((2, 2, PAD, KDIM), bf),
            vm((4, 2, 2, PAD, HALF), bf),
            vm((4, 2, 2, PAD, HALF), bf),
            vm((2, 2, 2, 2 * PAD, 4 * PAD), F32),
            vm((2, 2, 2 * PAD, 4 * PAD), F32),
            vm((2, 2, PAD, 4 * PAD), F32),
            vm((4, PAD, 4 * PAD), F32),
            vm((3, PAD, 4 * PAD), F32),
            vm((PAD, 4 * PAD), F32),
            vm((BLOCKS, CUT, 256), F32),
            dma((4, 2)), dma((4, 2)), dma((2, 4, 2)), dma((2, 4, 2)), dma((2, 4, 3)), dma((2, 4, 3)),
            dma((2,)), dma, dma, dma, dma, dma((4, 2)), dma((4, 2)),
            dma((2,)), dma((2,)), dma((2,)), dma((2,)),
            dma((4,)), dma((3,)), dma((4,)), dma((4,)),
            pltpu.SemaphoreType.REGULAR,
        ],
        compiler_params=pltpu.CompilerParams(
            collective_id=0, has_side_effects=True, vmem_limit_bytes=60 * 2**20
        ),
    )(responses, eigvecs)
    zl = lax.axis_index("exc") // 8
    c = lax.axis_index("unk") % 2
    mine = lax.dynamic_slice(gram, (0, c * 5, zl * 64), (BLOCKS, 45, 2 * PAD))
    mine = mine.reshape(BLOCKS, 45, 2, PAD)[..., :ROWS]
    return jnp.transpose(mine, (2, 0, 3, 1)), basis[:, :, :ROWS]


def solution(mesh):
    specs = P(None, None, "exc", "unk")
    return jax.shard_map(local, mesh=mesh, in_specs=(specs, P("exc", None)), out_specs=(specs, specs), check_vma=False)
```

```python
import jax
import jax.numpy as jnp
from jax import lax
from jax.experimental import pallas as pl
from jax.experimental.pallas import tpu as pltpu
from jax.sharding import PartitionSpec as P

MESH = pl.DeviceIdType.MESH
ROWS, PAD, HALF = 90, 96, 256
BLOCKS, RING, GROUPS = 4, 8, 16
WAVES = ROWS * GROUPS
KDIM = PAD * GROUPS
ZL_SLOT, ZH_SLOT = 1, 1
HROWS, HPAD = 45, 48
F32 = jnp.float32


def mod(value, size):
    return lax.rem(value + 2 * size, size)


def device(x, y, zh, zl, c):
    return {"exc": zl * 8 + y, "unk": (zh * 4 + x) * 2 + c}


def row_of(k):
    return k - 4 * (k // 3)


def col_of(k, s):
    plus = jnp.where((k == 0) | (k == 3), 1, 0)
    return plus * (k // 3 + s) - (1 - plus) * (k // 2 + s)


def kernel(
    x_ref, e_ref, basis_ref, gram_ref,
    xs, staged, window, ee, bsend, bland, parts, core_in, zl_in, zsum, zh_in, done, fin_in,
    scat_s, scat_r, near_s, near_r, ring_s, ring_r, win_s, eig_s, eig_r, fwd_s, fwd_r, out_s, out_r,
    core_s, core_r, zl_s, zl_r, zh_s, zh_r, fin_s, fin_r, above,
):
    exc, unk = lax.axis_index("exc"), lax.axis_index("unk")
    zl, y = exc // 8, exc % 8
    zh, x, c = unk // 8, (unk // 2) % 4, unk % 2
    other = 1 - zl
    up, down = device(x, mod(y + 1, 8), zh, zl, c), device(x, mod(y - 1, 8), zh, zl, c)
    pair = device(x, y, zh, other, c)
    sibling = device(x, y, zh, zl, 1 - c)
    pool = [(o, t) for o in (0, 1, 3, 2) for t in (1, 0) if (o, t) != (0, 0)]

    def pooled(o, t):
        return device(mod(x + o, 4), y, zh, (zl, other)[t], c)

    final_x, final_y, final_zh, is_self = [], [], [], []
    for n in range(2):
        k = 2 * n + zh // 2
        jy, iy = mod(y + row_of(k), 8), mod(y + col_of(k, c), 8)
        final_x.append(jy % 4)
        final_y.append(iy)
        final_zh.append(zl * 2 + jy // 4)
        here = (final_x[n] == x) & (iy == y) & (final_zh[n] == zh) & (zh % 2 == c)
        is_self.append([here & (zl == zi) for zi in (0, 1)])

    def remote(src, dst, send, recv, to):
        return pltpu.make_async_remote_copy(
            src_ref=src, dst_ref=dst, send_sem=send, recv_sem=recv, device_id=to, device_id_type=MESH
        )

    def win_copy(part):
        first = pl.multiple_of((part * 4 + x) * 1408 + part * 128, 128)
        return pltpu.make_async_copy(e_ref.at[:, pl.ds(first, KDIM)], window.at[part], win_s.at[part])

    win_copy(0).start()
    win_copy(1).start()

    barrier = pltpu.get_barrier_semaphore()

    def greet(to):
        pl.semaphore_signal(barrier, inc=1, device_id=to, device_id_type=MESH)

    around = [up, down, sibling] + [pooled(o, t) for o, t in pool]
    for to in around:
        greet(to)
    for k in (1, 2, 3):
        pl.when(zh < k)(lambda k=k: greet(device(x, y, k, zl, c)))
    pl.semaphore_wait(barrier, len(around) + zh)
    for k in (0, 1, 2):

        @pl.when(zh > k)
        def _():
            pl.semaphore_signal(above, inc=1, device_id=device(x, y, k, zl, c), device_id_type=MESH)

    def scat_copy(o, t):
        return remote(staged.at[mod(x + o, 4), t], xs.at[x, zl, y], scat_s.at[o, t], scat_r.at[x, zl], pooled(o, t))

    def scat_recv(o, t):
        q, z = mod(x + o, 4), (zl, other)[t]
        return remote(staged.at[q, t], xs.at[q, z, y], scat_s.at[o, t], scat_r.at[q, z], pooled(o, t))

    def near(way, o, t):
        q, z = mod(x + o, 4), (zl, other)[t]
        ref = xs.at[q, z, y]
        return remote(ref, ref, near_s.at[way, o, t], near_r.at[way, q, z], (up, down)[way])

    def near_recv(way, o, z):
        q = mod(x + o, 4)
        ref = xs.at[q, z, mod(y - 1, 8) if way == 0 else mod(y + 1, 8)]
        return remote(ref, ref, near_s.at[way, o, z], near_r.at[way, q, z], (up, down)[way])

    def ring_ref(way, o, d, hop):
        src = mod(y - hop, 8) if way == 0 else mod(y + hop, 8)
        q = mod(x + o, 4)
        return xs.at[q, :, src] if d < 4 else xs.at[q, way, src]

    def ring(way, o, d):
        ref = ring_ref(way, o, d, d - 1)
        return remote(ref, ref, ring_s.at[way, o, d - 2], ring_r.at[way, o, d - 2], (up, down)[way])

    def ring_recv(way, o, d):
        ref = ring_ref(way, o, d, d)
        return remote(ref, ref, ring_s.at[way, o, d - 2], ring_r.at[way, o, d - 2], (up, down)[way])

    staged[...] = jnp.zeros(staged.shape, jnp.bfloat16)
    for b in range(BLOCKS):
        for h in range(2):
            p, q = [x_ref[part, h * HROWS : (h + 1) * HROWS, b, :] for part in range(2)]
            low = jnp.concatenate([p[:, :HALF], q[:, :HALF]], axis=1)
            high = jnp.concatenate([p[:, HALF:], q[:, HALF:]], axis=1)
            first = jnp.full(low.shape, zl, jnp.int32) == 0
            staged[b, 0, h * HPAD : h * HPAD + HROWS, :] = jnp.where(first, low, high)
            staged[b, 1, h * HPAD : h * HPAD + HROWS, :] = jnp.where(first, high, low)
    scat_copy(0, 1).start()
    xs[x, zl, y] = staged[x, 0]
    near(0, 0, 0).start()
    near(1, 0, 0).start()
    for o, t in pool[1:]:
        scat_copy(o, t).start()

    def pack_eig():
        win_copy(0).wait()
        win_copy(1).wait()
        for part in range(2):
            ee[0, part] = jnp.zeros((PAD, KDIM), jnp.bfloat16)
        for at in range(4):

            @pl.when(x == at)
            def _():
                for part in range(2):
                    for i in range(2 * GROUPS):
                        first = at * 32 + i * HROWS
                        ee[0, part, 0:ROWS, i * HPAD : i * HPAD + HROWS] = window[part, :, first : first + HROWS]

    def eig_copy():
        return remote(ee.at[0, c], ee.at[1, c], eig_s, eig_r, pair)

    def eig_forward():
        return remote(ee.at[1, c], ee.at[1, c], fwd_s, fwd_r, sibling)

    def eig_forward_recv():
        return remote(ee.at[1, 1 - c], ee.at[1, 1 - c], fwd_s, fwd_r, sibling)

    def gram_partial(n, o):
        q = mod(x + o, 4)

        def one(t, _):
            k, s = 2 * n + t // 2, t % 2
            rows = xs[q, :, mod(y + row_of(k), 8)].reshape(2 * PAD, 2 * HALF)
            cols = []
            for zi in range(2):
                v = xs[q, zi, mod(y + col_of(k, s), 8)]
                cols += [v, jnp.concatenate([-v[:, HALF:], v[:, :HALF]], axis=1)]
            right = jnp.concatenate(cols, axis=0)
            parts[k, s] += lax.dot_general(rows, right, (((1,), (1,)), ((), ())), preferred_element_type=F32)
            return 0

        lax.fori_loop(0, 4, one, 0)

    def core_copy(k):
        return remote(parts.at[k, 1 - c], core_in.at[k], core_s.at[k], core_r.at[k], sibling)

    def zl_copy(k):
        rows = pl.ds(pl.multiple_of(other * PAD, PAD), PAD)
        return remote(parts.at[k, c, rows], zl_in.at[k], zl_s.at[k], zl_r.at[k], pair)

    def zh_copy(k, h):
        to = (k % 2) * 2 + h
        slot = mod(zh - to, 4) - 1
        return remote(
            zsum.at[k, h * HPAD : (h + 1) * HPAD], zh_in.at[k // 2, slot],
            zh_s.at[k, h], zh_r.at[k // 2, slot], device(x, y, to, zl, c),
        )

    def zh_recv(n, slot):
        return remote(zsum.at[0, 0:HPAD], zh_in.at[n, slot], zh_s.at[0, 0], zh_r.at[n, slot], sibling)

    def stage_core(k):
        core_copy(k).wait_recv()
        parts[k, c] += core_in[k]
        zl_copy(k).start()

    def stage_zl(k):
        zl_copy(k).wait_recv()
        zsum[k] = parts[k, c, pl.ds(pl.multiple_of(zl * PAD, PAD), PAD)] + zl_in[k]
        for h in (0, 1):
            pl.when(zh != (k % 2) * 2 + h)(lambda h=h: zh_copy(k, h).start())

    def fin_refs(n, zi):
        return done.at[n, :, zi * 128 : zi * 128 + 256], fin_in.at[x]

    def fin_copy(n, zi):
        src, dst = fin_refs(n, zi)
        to = device(final_x[n], final_y[n], final_zh[n], zi, zh % 2)
        return remote(src, dst, fin_s.at[n, zi], fin_r.at[x], to)

    def stage_zh(n):
        for slot in range(3):
            zh_recv(n, slot).wait_recv()
        rows = pl.ds(pl.multiple_of((zh % 2) * HPAD, HPAD), HPAD)
        done[n] = zsum[2 * n + zh // 2, rows] + zh_in[n, 0] + zh_in[n, 1] + zh_in[n, 2]
        for zi in (0, 1):
            pl.when(is_self[n][zi])(lambda zi=zi: pltpu.make_async_copy(*fin_refs(n, zi), fin_r.at[x]).start())
            pl.when(jnp.logical_not(is_self[n][zi]))(lambda zi=zi: fin_copy(n, zi).start())

    def stage_fin():
        left = jnp.full((HROWS, HROWS), zl, jnp.int32) == 0
        for b in range(BLOCKS):
            remote(done.at[0, :, 0:256], fin_in.at[b], fin_s.at[0, 0], fin_r.at[b], sibling).wait_recv()
            v = fin_in[b, 0:HROWS] * (1.0 / 16384.0)
            for part in range(2):
                for h in range(2):
                    at = part * PAD + h * HPAD
                    gram_ref[part, :, b, h * HROWS : (h + 1) * HROWS] = jnp.where(
                        left, v[:, at : at + HROWS], v[:, 64 + at : 64 + at + HROWS]
                    )

    mine = pl.ds(pl.multiple_of(zl * HALF, HALF), HALF)
    theirs = pl.ds(pl.multiple_of(other * HALF, HALF), HALF)

    def put(b, lanes, rows):
        for at in range(BLOCKS):

            @pl.when(b == at)
            def _():
                for part in range(2):
                    basis_ref[part, :, at, lanes] = rows[part, 0:ROWS]

    def out_copy(o, t):
        to = device(mod(x + o, 4), y, zh, zl + t * (other - zl), c)
        return remote(bsend.at[o, t], bland.at[x, zl], out_s.at[o, t], out_r.at[x, zl], to)

    def out_recv(o, t):
        b, half = mod(x + o, 4), (zl, other)[t]
        return remote(bsend.at[o, t], bland.at[b, half], out_s.at[o, t], out_r.at[b, half], pooled(o, t))

    def basis(o):
        q = mod(x + o, 4)

        def rows_of(n, _):
            t = 1 - n
            prod = jnp.dot(ee[t].reshape(2 * PAD, KDIM), xs[q].reshape(KDIM, 2 * HALF), preferred_element_type=F32)
            bsend[o, t, 0] = (prod[:PAD, :HALF] - prod[PAD:, HALF:]).astype(jnp.bfloat16)
            bsend[o, t, 1] = (prod[PAD:, :HALF] + prod[:PAD, HALF:]).astype(jnp.bfloat16)
            own = (o == 0) & (t == 0)

            @pl.when(own)
            def _():
                put(x, mine, bsend.at[0, 0])

            pl.when(jnp.logical_not(own))(lambda: out_copy(o, t).start())
            return 0

        lax.fori_loop(0, 2, rows_of, 0)

    def basis_land(o, t):
        out_recv(o, t).wait_recv()
        b, half = mod(x + o, 4), (zl, other)[t]
        put(b, (mine, theirs)[t], bland.at[b, half])

    for o in (0, 3, 1, 2):
        for t in (0, 1):
            if (o, t) != (0, 0):
                scat_recv(o, t).wait_recv()
                near(0, o, t).start()
                near(1, o, t).start()
    pack_eig()
    eig_copy().start()
    parts[...] = jnp.zeros(parts.shape, F32)

    def hop_one(i, _):
        o = jnp.where(i == 0, 0, jnp.where(i == 1, 3, i - 1))
        for way in (0, 1):
            near_recv(way, o, 0).wait_recv()
            near_recv(way, o, 1).wait_recv()
            ring(way, o, 2).start()
        gram_partial(0, o)
        return 0

    def hop_two(i, _):
        o = jnp.where(i == 0, 0, jnp.where(i == 1, 3, i - 1))
        for way in (0, 1):
            ring_recv(way, o, 2).wait_recv()
            ring(way, o, 3).start()
        gram_partial(1, o)

        @pl.when(i == 2)
        def _():
            pl.when(zh < 3)(lambda: pl.semaphore_wait(above, 3 - zh))
            stage_zl(0)
            stage_zl(1)

        return 0

    def hop_three(i, _):
        o = jnp.where(i == 0, 0, jnp.where(i == 1, 3, i - 1))
        for way in (0, 1):
            ring_recv(way, o, 3).wait_recv()
            ring(way, o, 4).start()

        @pl.when(i == 0)
        def _():
            eig_copy().wait_recv()
            eig_forward().start()

        pl.when(i == ZL_SLOT)(lambda: stage_zl(2))

        @pl.when(i == ZL_SLOT + 1)
        def _():
            stage_zl(3)
            stage_zh(0)

        return 0

    def hop_four(i, _):
        o = jnp.where(i == 0, 3, jnp.where(i == 3, 0, i))
        for way in (0, 1):
            ring_recv(way, o, 4).wait_recv()
        basis(o)
        pl.when(i == ZH_SLOT + zh // 2)(lambda: stage_zh(1))
        return 0

    lax.fori_loop(0, 4, hop_one, 0)
    for k in (0, 1):
        core_copy(k).start()
    for k in (0, 1):
        stage_core(k)
    lax.fori_loop(0, 4, hop_two, 0)
    for k in (2, 3):
        core_copy(k).start()
    for k in (2, 3):
        stage_core(k)
    lax.fori_loop(0, 4, hop_three, 0)
    eig_forward_recv().wait_recv()
    lax.fori_loop(0, 4, hop_four, 0)
    for o in (1, 3, 2):
        for t in (0, 1):
            basis_land(o, t)
    stage_fin()
    basis_land(0, 1)

    for o, t in pool:
        scat_copy(o, t).wait_send()
        out_copy(o, t).wait_send()
    for way in (0, 1):
        for o in range(4):
            near(way, o, 0).wait_send()
            near(way, o, 1).wait_send()
            for d in (2, 3, 4):
                ring(way, o, d).wait_send()
    eig_copy().wait_send()
    eig_forward().wait_send()
    for k in range(4):
        core_copy(k).wait_send()
        zl_copy(k).wait_send()
        for h in (0, 1):
            pl.when(zh != (k % 2) * 2 + h)(lambda k=k, h=h: zh_copy(k, h).wait_send())
    for n in range(2):
        for zi in (0, 1):
            pl.when(jnp.logical_not(is_self[n][zi]))(lambda n=n, zi=zi: fin_copy(n, zi).wait_send())


def hand_on(basis_ref, gram_ref, basis_out, gram_out, basis_sem, gram_sem):
    copies = []
    for part in range(2):
        copies.append(pltpu.make_async_copy(basis_ref.at[part], basis_out.at[part], basis_sem.at[part]))
        copies.append(pltpu.make_async_copy(gram_ref.at[part], gram_out.at[part], gram_sem.at[part]))
    for copy in copies:
        copy.start()
    for copy in copies:
        copy.wait()


def local(responses, eigvecs):
    dma = pltpu.SemaphoreType.DMA
    bf, vm = jnp.bfloat16, pltpu.VMEM
    basis, gram = pl.pallas_call(
        kernel,
        out_shape=(
            jax.ShapeDtypeStruct((2, ROWS, BLOCKS, 2 * HALF), bf),
            jax.ShapeDtypeStruct((2, 45, BLOCKS, ROWS), F32),
        ),
        in_specs=[pl.BlockSpec(memory_space=vm), pl.BlockSpec(memory_space=pl.ANY)],
        out_specs=(pl.BlockSpec(memory_space=vm),) * 2,
        scratch_shapes=[
            vm((4, 2, RING, PAD, 2 * HALF), bf),
            vm((4, 2, PAD, 2 * HALF), bf),
            vm((2, ROWS, KDIM), bf),
            vm((2, 2, PAD, KDIM), bf),
            vm((4, 2, 2, PAD, HALF), bf),
            vm((4, 2, 2, PAD, HALF), bf),
            vm((4, 2, 2 * PAD, 4 * PAD), F32),
            vm((4, 2 * PAD, 4 * PAD), F32),
            vm((4, PAD, 4 * PAD), F32),
            vm((4, PAD, 4 * PAD), F32),
            vm((2, 3, HPAD, 4 * PAD), F32),
            vm((2, HPAD, 4 * PAD), F32),
            vm((BLOCKS, HPAD, 256), F32),
            dma((4, 2)), dma((4, 2)), dma((2, 4, 2)), dma((2, 4, 2)), dma((2, 4, 3)), dma((2, 4, 3)),
            dma((2,)), dma, dma, dma, dma, dma((4, 2)), dma((4, 2)),
            dma((4,)), dma((4,)), dma((4,)), dma((4,)),
            dma((4, 2)), dma((2, 3)), dma((2, 2)), dma((4,)),
            pltpu.SemaphoreType.REGULAR,
        ],
        compiler_params=pltpu.CompilerParams(
            collective_id=0, has_side_effects=True, vmem_limit_bytes=60 * 2**20
        ),
    )(jnp.transpose(responses, (0, 2, 1, 3)), eigvecs)
    basis, gram = pl.pallas_call(
        hand_on,
        out_shape=(jax.ShapeDtypeStruct(basis.shape, bf), jax.ShapeDtypeStruct(gram.shape, F32)),
        in_specs=[pl.BlockSpec(memory_space=vm)] * 2,
        out_specs=(pl.BlockSpec(memory_space=pl.ANY),) * 2,
        scratch_shapes=[dma((2,)), dma((2,))],
    )(basis, gram)
    return jnp.transpose(gram, (0, 2, 3, 1)), jnp.transpose(basis, (0, 2, 1, 3))


def solution(mesh):
    specs = P(None, None, "exc", "unk")
    return jax.shard_map(local, mesh=mesh, in_specs=(specs, P("exc", None)), out_specs=(specs, specs), check_vma=False)
```

```python
import jax
import jax.numpy as jnp
from jax import lax
from jax.experimental import pallas as pl
from jax.experimental.pallas import tpu as pltpu
from jax.sharding import PartitionSpec as P

MESH = pl.DeviceIdType.MESH
ROWS, PAD, HALF = 90, 96, 256
BLOCKS, RING, GROUPS = 4, 8, 16
WAVES = ROWS * GROUPS
KDIM = PAD * GROUPS
ZL_SLOT, ZH_SLOT = 1, 1
HROWS, HPAD = 45, 48
F32 = jnp.float32


def mod(value, size):
    return lax.rem(value + 2 * size, size)


def device(x, y, zh, zl, c):
    return {"exc": zl * 8 + y, "unk": (zh * 4 + x) * 2 + c}


def row_of(k):
    return k - 4 * (k // 3)


def col_of(k, s):
    plus = jnp.where((k == 0) | (k == 3), 1, 0)
    return plus * (k // 3 + s) - (1 - plus) * (k // 2 + s)


def kernel(
    x_hbm, e_ref, basis_ref, gram_ref,
    x_ref, xs, staged, window, ee, bsend, bland, parts, core_in, zl_in, zsum, zh_in, done, fin_in,
    x_sem, scat_s, scat_r, near_s, near_r, ring_s, ring_r, win_s, eig_s, eig_r, fwd_s, fwd_r, out_s, out_r,
    core_s, core_r, zl_s, zl_r, zh_s, zh_r, fin_s, fin_r, above,
):
    exc, unk = lax.axis_index("exc"), lax.axis_index("unk")
    zl, y = exc // 8, exc % 8
    zh, x, c = unk // 8, (unk // 2) % 4, unk % 2
    other = 1 - zl
    up, down = device(x, mod(y + 1, 8), zh, zl, c), device(x, mod(y - 1, 8), zh, zl, c)
    pair = device(x, y, zh, other, c)
    sibling = device(x, y, zh, zl, 1 - c)
    pool = [(o, t) for o in (0, 1, 3, 2) for t in (1, 0) if (o, t) != (0, 0)]

    def pooled(o, t):
        return device(mod(x + o, 4), y, zh, (zl, other)[t], c)

    final_x, final_y, final_zh, is_self = [], [], [], []
    for n in range(2):
        k = 2 * n + zh // 2
        jy, iy = mod(y + row_of(k), 8), mod(y + col_of(k, c), 8)
        final_x.append(jy % 4)
        final_y.append(iy)
        final_zh.append(zl * 2 + jy // 4)
        here = (final_x[n] == x) & (iy == y) & (final_zh[n] == zh) & (zh % 2 == c)
        is_self.append([here & (zl == zi) for zi in (0, 1)])

    def remote(src, dst, send, recv, to):
        return pltpu.make_async_remote_copy(
            src_ref=src, dst_ref=dst, send_sem=send, recv_sem=recv, device_id=to, device_id_type=MESH
        )

    def win_copy(part):
        first = pl.multiple_of((part * 4 + x) * 1408 + part * 128, 128)
        return pltpu.make_async_copy(e_ref.at[:, pl.ds(first, KDIM)], window.at[part], win_s.at[part])

    x_copies = [pltpu.make_async_copy(x_hbm.at[part], x_ref.at[part], x_sem.at[part]) for part in range(2)]
    for copy in x_copies:
        copy.start()
    win_copy(0).start()
    win_copy(1).start()

    barrier = pltpu.get_barrier_semaphore()

    def greet(to):
        pl.semaphore_signal(barrier, inc=1, device_id=to, device_id_type=MESH)

    around = [up, down, sibling] + [pooled(o, t) for o, t in pool]
    for to in around:
        greet(to)
    for k in (1, 2, 3):
        pl.when(zh < k)(lambda k=k: greet(device(x, y, k, zl, c)))

    def scat_copy(o, t):
        return remote(staged.at[mod(x + o, 4), t], xs.at[x, zl, y], scat_s.at[o, t], scat_r.at[x, zl], pooled(o, t))

    def scat_recv(o, t):
        q, z = mod(x + o, 4), (zl, other)[t]
        return remote(staged.at[q, t], xs.at[q, z, y], scat_s.at[o, t], scat_r.at[q, z], pooled(o, t))

    def near(way, o, t):
        q, z = mod(x + o, 4), (zl, other)[t]
        ref = xs.at[q, z, y]
        return remote(ref, ref, near_s.at[way, o, t], near_r.at[way, q, z], (up, down)[way])

    def near_recv(way, o, z):
        q = mod(x + o, 4)
        ref = xs.at[q, z, mod(y - 1, 8) if way == 0 else mod(y + 1, 8)]
        return remote(ref, ref, near_s.at[way, o, z], near_r.at[way, q, z], (up, down)[way])

    def ring_ref(way, o, d, hop):
        src = mod(y - hop, 8) if way == 0 else mod(y + hop, 8)
        q = mod(x + o, 4)
        return xs.at[q, :, src] if d < 4 else xs.at[q, way, src]

    def ring(way, o, d):
        ref = ring_ref(way, o, d, d - 1)
        return remote(ref, ref, ring_s.at[way, o, d - 2], ring_r.at[way, o, d - 2], (up, down)[way])

    def ring_recv(way, o, d):
        ref = ring_ref(way, o, d, d)
        return remote(ref, ref, ring_s.at[way, o, d - 2], ring_r.at[way, o, d - 2], (up, down)[way])

    staged[...] = jnp.zeros(staged.shape, jnp.bfloat16)
    for copy in x_copies:
        copy.wait()
    for b in range(BLOCKS):
        for h in range(2):
            p, q = [x_ref[part, h * HROWS : (h + 1) * HROWS, b, :] for part in range(2)]
            low = jnp.concatenate([p[:, :HALF], q[:, :HALF]], axis=1)
            high = jnp.concatenate([p[:, HALF:], q[:, HALF:]], axis=1)
            first = jnp.full(low.shape, zl, jnp.int32) == 0
            staged[b, 0, h * HPAD : h * HPAD + HROWS, :] = jnp.where(first, low, high)
            staged[b, 1, h * HPAD : h * HPAD + HROWS, :] = jnp.where(first, high, low)
    xs[x, zl, y] = staged[x, 0]

    pl.semaphore_wait(barrier, len(around) + zh)
    for k in (0, 1, 2):

        @pl.when(zh > k)
        def _():
            pl.semaphore_signal(above, inc=1, device_id=device(x, y, k, zl, c), device_id_type=MESH)

    scat_copy(0, 1).start()
    near(0, 0, 0).start()
    near(1, 0, 0).start()
    for o, t in pool[1:]:
        scat_copy(o, t).start()

    def pack_eig():
        win_copy(0).wait()
        win_copy(1).wait()
        for part in range(2):
            ee[0, part] = jnp.zeros((PAD, KDIM), jnp.bfloat16)
        for at in range(4):

            @pl.when(x == at)
            def _():
                for part in range(2):
                    for i in range(2 * GROUPS):
                        first = at * 32 + i * HROWS
                        ee[0, part, 0:ROWS, i * HPAD : i * HPAD + HROWS] = window[part, :, first : first + HROWS]

    def eig_copy():
        return remote(ee.at[0, c], ee.at[1, c], eig_s, eig_r, pair)

    def eig_forward():
        return remote(ee.at[1, c], ee.at[1, c], fwd_s, fwd_r, sibling)

    def eig_forward_recv():
        return remote(ee.at[1, 1 - c], ee.at[1, 1 - c], fwd_s, fwd_r, sibling)

    def gram_partial(n, o):
        q = mod(x + o, 4)

        def one(t, _):
            k, s = 2 * n + t // 2, t % 2
            rows = xs[q, :, mod(y + row_of(k), 8)].reshape(2 * PAD, 2 * HALF)
            cols = []
            for zi in range(2):
                v = xs[q, zi, mod(y + col_of(k, s), 8)]
                cols += [v, jnp.concatenate([-v[:, HALF:], v[:, :HALF]], axis=1)]
            right = jnp.concatenate(cols, axis=0)
            parts[k, s] += lax.dot_general(rows, right, (((1,), (1,)), ((), ())), preferred_element_type=F32)
            return 0

        lax.fori_loop(0, 4, one, 0)

    def core_copy(k):
        return remote(parts.at[k, 1 - c], core_in.at[k], core_s.at[k], core_r.at[k], sibling)

    def zl_copy(k):
        rows = pl.ds(pl.multiple_of(other * PAD, PAD), PAD)
        return remote(parts.at[k, c, rows], zl_in.at[k], zl_s.at[k], zl_r.at[k], pair)

    def zh_copy(k, h):
        to = (k % 2) * 2 + h
        slot = mod(zh - to, 4) - 1
        return remote(
            zsum.at[k, h * HPAD : (h + 1) * HPAD], zh_in.at[k // 2, slot],
            zh_s.at[k, h], zh_r.at[k // 2, slot], device(x, y, to, zl, c),
        )

    def zh_recv(n, slot):
        return remote(zsum.at[0, 0:HPAD], zh_in.at[n, slot], zh_s.at[0, 0], zh_r.at[n, slot], sibling)

    def stage_core(k):
        core_copy(k).wait_recv()
        parts[k, c] += core_in[k]
        zl_copy(k).start()

    def stage_zl(k):
        zl_copy(k).wait_recv()
        zsum[k] = parts[k, c, pl.ds(pl.multiple_of(zl * PAD, PAD), PAD)] + zl_in[k]
        for h in (0, 1):
            pl.when(zh != (k % 2) * 2 + h)(lambda h=h: zh_copy(k, h).start())

    def fin_refs(n, zi):
        return done.at[n, :, zi * 128 : zi * 128 + 256], fin_in.at[x]

    def fin_copy(n, zi):
        src, dst = fin_refs(n, zi)
        to = device(final_x[n], final_y[n], final_zh[n], zi, zh % 2)
        return remote(src, dst, fin_s.at[n, zi], fin_r.at[x], to)

    def stage_zh(n):
        for slot in range(3):
            zh_recv(n, slot).wait_recv()
        rows = pl.ds(pl.multiple_of((zh % 2) * HPAD, HPAD), HPAD)
        done[n] = zsum[2 * n + zh // 2, rows] + zh_in[n, 0] + zh_in[n, 1] + zh_in[n, 2]
        for zi in (0, 1):
            pl.when(is_self[n][zi])(lambda zi=zi: pltpu.make_async_copy(*fin_refs(n, zi), fin_r.at[x]).start())
            pl.when(jnp.logical_not(is_self[n][zi]))(lambda zi=zi: fin_copy(n, zi).start())

    def stage_fin():
        left = jnp.full((HROWS, HROWS), zl, jnp.int32) == 0
        for b in range(BLOCKS):
            remote(done.at[0, :, 0:256], fin_in.at[b], fin_s.at[0, 0], fin_r.at[b], sibling).wait_recv()
            v = fin_in[b, 0:HROWS] * (1.0 / 16384.0)
            for part in range(2):
                for h in range(2):
                    at = part * PAD + h * HPAD
                    gram_ref[part, :, b, h * HROWS : (h + 1) * HROWS] = jnp.where(
                        left, v[:, at : at + HROWS], v[:, 64 + at : 64 + at + HROWS]
                    )

    mine = pl.ds(pl.multiple_of(zl * HALF, HALF), HALF)
    theirs = pl.ds(pl.multiple_of(other * HALF, HALF), HALF)

    def put(b, lanes, rows):
        for at in range(BLOCKS):

            @pl.when(b == at)
            def _():
                for part in range(2):
                    basis_ref[part, :, at, lanes] = rows[part, 0:ROWS]

    def out_copy(o, t):
        to = device(mod(x + o, 4), y, zh, zl + t * (other - zl), c)
        return remote(bsend.at[o, t], bland.at[x, zl], out_s.at[o, t], out_r.at[x, zl], to)

    def out_recv(o, t):
        b, half = mod(x + o, 4), (zl, other)[t]
        return remote(bsend.at[o, t], bland.at[b, half], out_s.at[o, t], out_r.at[b, half], pooled(o, t))

    def basis(o):
        q = mod(x + o, 4)

        def rows_of(n, _):
            t = 1 - n
            prod = jnp.dot(ee[t].reshape(2 * PAD, KDIM), xs[q].reshape(KDIM, 2 * HALF), preferred_element_type=F32)
            bsend[o, t, 0] = (prod[:PAD, :HALF] - prod[PAD:, HALF:]).astype(jnp.bfloat16)
            bsend[o, t, 1] = (prod[PAD:, :HALF] + prod[:PAD, HALF:]).astype(jnp.bfloat16)
            own = (o == 0) & (t == 0)

            @pl.when(own)
            def _():
                put(x, mine, bsend.at[0, 0])

            pl.when(jnp.logical_not(own))(lambda: out_copy(o, t).start())
            return 0

        lax.fori_loop(0, 2, rows_of, 0)

    def basis_land(o, t):
        out_recv(o, t).wait_recv()
        b, half = mod(x + o, 4), (zl, other)[t]
        put(b, (mine, theirs)[t], bland.at[b, half])

    for o in (0, 3, 1, 2):
        for t in (0, 1):
            if (o, t) != (0, 0):
                scat_recv(o, t).wait_recv()
                near(0, o, t).start()
                near(1, o, t).start()
    pack_eig()
    eig_copy().start()
    parts[...] = jnp.zeros(parts.shape, F32)

    def hop_one(i, _):
        o = jnp.where(i == 0, 0, jnp.where(i == 1, 3, i - 1))
        for way in (0, 1):
            near_recv(way, o, 0).wait_recv()
            near_recv(way, o, 1).wait_recv()
            ring(way, o, 2).start()
        gram_partial(0, o)
        return 0

    def hop_two(i, _):
        o = jnp.where(i == 0, 0, jnp.where(i == 1, 3, i - 1))
        for way in (0, 1):
            ring_recv(way, o, 2).wait_recv()
            ring(way, o, 3).start()
        gram_partial(1, o)

        @pl.when(i == 2)
        def _():
            pl.when(zh < 3)(lambda: pl.semaphore_wait(above, 3 - zh))
            stage_zl(0)
            stage_zl(1)

        return 0

    def hop_three(i, _):
        o = jnp.where(i == 0, 0, jnp.where(i == 1, 3, i - 1))
        for way in (0, 1):
            ring_recv(way, o, 3).wait_recv()
            pl.when(i >= 2)(lambda way=way: ring(way, 3 - 2 * (i - 2), 4).start())

        @pl.when(i == 0)
        def _():
            eig_copy().wait_recv()
            eig_forward().start()

        pl.when(i == ZL_SLOT)(lambda: stage_zl(2))

        @pl.when(i == ZL_SLOT + 1)
        def _():
            stage_zl(3)
            stage_zh(0)

        return 0

    def hop_four(i, _):
        o = jnp.where(i == 0, 3, jnp.where(i == 3, 0, i))
        for way in (0, 1):
            ring_recv(way, o, 4).wait_recv()
            pl.when(i < 2)(lambda way=way: ring(way, 2 - 2 * i, 4).start())
        basis(o)
        pl.when(i == ZH_SLOT)(lambda: stage_zh(1))
        return 0

    lax.fori_loop(0, 4, hop_one, 0)
    for k in (0, 1):
        core_copy(k).start()
    for k in (0, 1):
        stage_core(k)
    lax.fori_loop(0, 4, hop_two, 0)
    for k in (2, 3):
        core_copy(k).start()
    for k in (2, 3):
        stage_core(k)
    lax.fori_loop(0, 4, hop_three, 0)
    eig_forward_recv().wait_recv()
    lax.fori_loop(0, 4, hop_four, 0)
    for o in (1, 3, 2):
        for t in (0, 1):
            basis_land(o, t)
    stage_fin()
    basis_land(0, 1)

    for o, t in pool:
        scat_copy(o, t).wait_send()
        out_copy(o, t).wait_send()
    for way in (0, 1):
        for o in range(4):
            near(way, o, 0).wait_send()
            near(way, o, 1).wait_send()
            for d in (2, 3, 4):
                ring(way, o, d).wait_send()
    eig_copy().wait_send()
    eig_forward().wait_send()
    for k in range(4):
        core_copy(k).wait_send()
        zl_copy(k).wait_send()
        for h in (0, 1):
            pl.when(zh != (k % 2) * 2 + h)(lambda k=k, h=h: zh_copy(k, h).wait_send())
    for n in range(2):
        for zi in (0, 1):
            pl.when(jnp.logical_not(is_self[n][zi]))(lambda n=n, zi=zi: fin_copy(n, zi).wait_send())


def hand_on(basis_ref, gram_ref, basis_out, gram_out, basis_sem, gram_sem):
    copies = []
    for part in range(2):
        copies.append(pltpu.make_async_copy(basis_ref.at[part], basis_out.at[part], basis_sem.at[part]))
        copies.append(pltpu.make_async_copy(gram_ref.at[part], gram_out.at[part], gram_sem.at[part]))
    for copy in copies:
        copy.start()
    for copy in copies:
        copy.wait()


def local(responses, eigvecs):
    dma = pltpu.SemaphoreType.DMA
    bf, vm = jnp.bfloat16, pltpu.VMEM
    basis, gram = pl.pallas_call(
        kernel,
        out_shape=(
            jax.ShapeDtypeStruct((2, ROWS, BLOCKS, 2 * HALF), bf),
            jax.ShapeDtypeStruct((2, 45, BLOCKS, ROWS), F32),
        ),
        in_specs=[pl.BlockSpec(memory_space=pl.ANY)] * 2,
        out_specs=(pl.BlockSpec(memory_space=vm),) * 2,
        scratch_shapes=[
            vm((2, ROWS, BLOCKS, 2 * HALF), bf),
            vm((4, 2, RING, PAD, 2 * HALF), bf),
            vm((4, 2, PAD, 2 * HALF), bf),
            vm((2, ROWS, KDIM), bf),
            vm((2, 2, PAD, KDIM), bf),
            vm((4, 2, 2, PAD, HALF), bf),
            vm((4, 2, 2, PAD, HALF), bf),
            vm((4, 2, 2 * PAD, 4 * PAD), F32),
            vm((4, 2 * PAD, 4 * PAD), F32),
            vm((4, PAD, 4 * PAD), F32),
            vm((4, PAD, 4 * PAD), F32),
            vm((2, 3, HPAD, 4 * PAD), F32),
            vm((2, HPAD, 4 * PAD), F32),
            vm((BLOCKS, HPAD, 256), F32),
            dma((2,)), dma((4, 2)), dma((4, 2)), dma((2, 4, 2)), dma((2, 4, 2)), dma((2, 4, 3)), dma((2, 4, 3)),
            dma((2,)), dma, dma, dma, dma, dma((4, 2)), dma((4, 2)),
            dma((4,)), dma((4,)), dma((4,)), dma((4,)),
            dma((4, 2)), dma((2, 3)), dma((2, 2)), dma((4,)),
            pltpu.SemaphoreType.REGULAR,
        ],
        compiler_params=pltpu.CompilerParams(
            collective_id=0, has_side_effects=True, vmem_limit_bytes=60 * 2**20
        ),
    )(jnp.transpose(responses, (0, 2, 1, 3)), eigvecs)
    basis, gram = pl.pallas_call(
        hand_on,
        out_shape=(jax.ShapeDtypeStruct(basis.shape, bf), jax.ShapeDtypeStruct(gram.shape, F32)),
        in_specs=[pl.BlockSpec(memory_space=vm)] * 2,
        out_specs=(pl.BlockSpec(memory_space=pl.ANY),) * 2,
        scratch_shapes=[dma((2,)), dma((2,))],
    )(basis, gram)
    return jnp.transpose(gram, (0, 2, 3, 1)), jnp.transpose(basis, (0, 2, 1, 3))


def solution(mesh):
    specs = P(None, None, "exc", "unk")
    return jax.shard_map(local, mesh=mesh, in_specs=(specs, P("exc", None)), out_specs=(specs, specs), check_vma=False)
```

```python
import jax
import jax.numpy as jnp
from jax import lax
from jax.experimental import pallas as pl
from jax.experimental.pallas import tpu as pltpu
from jax.sharding import PartitionSpec as P

MESH = pl.DeviceIdType.MESH
ROWS, PAD, HALF = 90, 96, 256
BLOCKS, RING, GROUPS = 4, 8, 16
WAVES = ROWS * GROUPS
KDIM = PAD * GROUPS
ZL_SLOT, ZH_SLOT = 0, 1
HROWS, HPAD = 45, 48
F32 = jnp.float32


def mod(value, size):
    return lax.rem(value + 2 * size, size)


def device(x, y, zh, zl, c):
    return {"exc": zl * 8 + y, "unk": (zh * 4 + x) * 2 + c}


def row_of(k):
    return k - 4 * (k // 3)


def col_of(k, s):
    plus = jnp.where((k == 0) | (k == 3), 1, 0)
    return plus * (k // 3 + s) - (1 - plus) * (k // 2 + s)


def kernel(
    x_hbm, e_ref, basis_ref, gram_ref,
    x_ref, xs, staged, window, ee, bsend, bland, parts, core_in, zl_in, zsum, zh_in, done, fin_in,
    x_sem, scat_s, scat_r, near_s, near_r, ring_s, ring_r, win_s, eig_s, eig_r, fwd_s, fwd_r, out_s, out_r,
    core_s, core_r, zl_s, zl_r, zh_s, zh_r, fin_s, fin_r, above,
):
    exc, unk = lax.axis_index("exc"), lax.axis_index("unk")
    zl, y = exc // 8, exc % 8
    zh, x, c = unk // 8, (unk // 2) % 4, unk % 2
    other = 1 - zl
    up, down = device(x, mod(y + 1, 8), zh, zl, c), device(x, mod(y - 1, 8), zh, zl, c)
    pair = device(x, y, zh, other, c)
    sibling = device(x, y, zh, zl, 1 - c)
    pool = [(o, t) for o in (0, 1, 3, 2) for t in (1, 0) if (o, t) != (0, 0)]

    def pooled(o, t):
        return device(mod(x + o, 4), y, zh, (zl, other)[t], c)

    final_x, final_y, final_zh, is_self = [], [], [], []
    for n in range(2):
        k = 2 * n + zh // 2
        jy, iy = mod(y + row_of(k), 8), mod(y + col_of(k, c), 8)
        final_x.append(jy % 4)
        final_y.append(iy)
        final_zh.append(zl * 2 + jy // 4)
        here = (final_x[n] == x) & (iy == y) & (final_zh[n] == zh) & (zh % 2 == c)
        is_self.append([here & (zl == zi) for zi in (0, 1)])

    def remote(src, dst, send, recv, to):
        return pltpu.make_async_remote_copy(
            src_ref=src, dst_ref=dst, send_sem=send, recv_sem=recv, device_id=to, device_id_type=MESH
        )

    def win_copy(part):
        first = pl.multiple_of((part * 4 + x) * 1408 + part * 128, 128)
        return pltpu.make_async_copy(e_ref.at[:, pl.ds(first, KDIM)], window.at[part], win_s.at[part])

    x_copies = [pltpu.make_async_copy(x_hbm.at[part], x_ref.at[part], x_sem.at[part]) for part in range(2)]
    for copy in x_copies:
        copy.start()
    win_copy(0).start()
    win_copy(1).start()

    barrier = pltpu.get_barrier_semaphore()

    def greet(to):
        pl.semaphore_signal(barrier, inc=1, device_id=to, device_id_type=MESH)

    around = [up, down, sibling] + [pooled(o, t) for o, t in pool]
    for to in around:
        greet(to)
    for k in (1, 2, 3):
        pl.when(zh < k)(lambda k=k: greet(device(x, y, k, zl, c)))

    def scat_copy(o, t):
        return remote(staged.at[mod(x + o, 4), t], xs.at[x, zl, y], scat_s.at[o, t], scat_r.at[x, zl], pooled(o, t))

    def scat_recv(o, t):
        q, z = mod(x + o, 4), (zl, other)[t]
        return remote(staged.at[q, t], xs.at[q, z, y], scat_s.at[o, t], scat_r.at[q, z], pooled(o, t))

    def near(way, o, t):
        q, z = mod(x + o, 4), (zl, other)[t]
        ref = xs.at[q, z, y]
        return remote(ref, ref, near_s.at[way, o, t], near_r.at[way, q, z], (up, down)[way])

    def near_recv(way, o, z):
        q = mod(x + o, 4)
        ref = xs.at[q, z, mod(y - 1, 8) if way == 0 else mod(y + 1, 8)]
        return remote(ref, ref, near_s.at[way, o, z], near_r.at[way, q, z], (up, down)[way])

    def ring_ref(way, o, d, hop):
        src = mod(y - hop, 8) if way == 0 else mod(y + hop, 8)
        q = mod(x + o, 4)
        return xs.at[q, :, src] if d < 4 else xs.at[q, way, src]

    def ring(way, o, d):
        ref = ring_ref(way, o, d, d - 1)
        return remote(ref, ref, ring_s.at[way, o, d - 2], ring_r.at[way, o, d - 2], (up, down)[way])

    def ring_recv(way, o, d):
        ref = ring_ref(way, o, d, d)
        return remote(ref, ref, ring_s.at[way, o, d - 2], ring_r.at[way, o, d - 2], (up, down)[way])

    staged[...] = jnp.zeros(staged.shape, jnp.bfloat16)
    for copy in x_copies:
        copy.wait()
    for b in range(BLOCKS):
        for h in range(2):
            p, q = [x_ref[part, h * HROWS : (h + 1) * HROWS, b, :] for part in range(2)]
            low = jnp.concatenate([p[:, :HALF], q[:, :HALF]], axis=1)
            high = jnp.concatenate([p[:, HALF:], q[:, HALF:]], axis=1)
            first = jnp.full(low.shape, zl, jnp.int32) == 0
            staged[b, 0, h * HPAD : h * HPAD + HROWS, :] = jnp.where(first, low, high)
            staged[b, 1, h * HPAD : h * HPAD + HROWS, :] = jnp.where(first, high, low)
    xs[x, zl, y] = staged[x, 0]

    pl.semaphore_wait(barrier, len(around) + zh)
    for k in (0, 1, 2):

        @pl.when(zh > k)
        def _():
            pl.semaphore_signal(above, inc=1, device_id=device(x, y, k, zl, c), device_id_type=MESH)

    scat_copy(0, 1).start()
    near(0, 0, 0).start()
    near(1, 0, 0).start()
    for o, t in pool[1:]:
        scat_copy(o, t).start()

    def pack_eig():
        win_copy(0).wait()
        win_copy(1).wait()
        for part in range(2):
            ee[0, part] = jnp.zeros((PAD, KDIM), jnp.bfloat16)
        for at in range(4):

            @pl.when(x == at)
            def _():
                for part in range(2):
                    for i in range(2 * GROUPS):
                        first = at * 32 + i * HROWS
                        ee[0, part, 0:ROWS, i * HPAD : i * HPAD + HROWS] = window[part, :, first : first + HROWS]

    def eig_copy():
        return remote(ee.at[0, c], ee.at[1, c], eig_s, eig_r, pair)

    def eig_forward():
        return remote(ee.at[1, c], ee.at[1, c], fwd_s, fwd_r, sibling)

    def eig_forward_recv():
        return remote(ee.at[1, 1 - c], ee.at[1, 1 - c], fwd_s, fwd_r, sibling)

    def gram_partial(n, o):
        q = mod(x + o, 4)

        def one(t, _):
            k, s = (t // 2 + t // 4, t % 2) if n == 0 else (2 + t // 2, t % 2 + t // 2)
            rows = xs[q, :, mod(y + row_of(k), 8)].reshape(2 * PAD, 2 * HALF)
            cols = []
            for zi in range(2):
                v = xs[q, zi, mod(y + col_of(k, s), 8)]
                cols += [v, jnp.concatenate([-v[:, HALF:], v[:, :HALF]], axis=1)]
            right = jnp.concatenate(cols, axis=0)
            parts[k, s] += lax.dot_general(rows, right, (((1,), (1,)), ((), ())), preferred_element_type=F32)
            return 0

        lax.fori_loop(0, 5 - 2 * n, one, 0)

    def core_copy(k):
        return remote(parts.at[k, 1 - c], core_in.at[k], core_s.at[k], core_r.at[k], sibling)

    def zl_copy(k):
        rows = pl.ds(pl.multiple_of(other * PAD, PAD), PAD)
        return remote(parts.at[k, c, rows], zl_in.at[k], zl_s.at[k], zl_r.at[k], pair)

    def zh_copy(k, h):
        to = (k % 2) * 2 + h
        slot = mod(zh - to, 4) - 1
        return remote(
            zsum.at[k, h * HPAD : (h + 1) * HPAD], zh_in.at[k // 2, slot],
            zh_s.at[k, h], zh_r.at[k // 2, slot], device(x, y, to, zl, c),
        )

    def zh_recv(n, slot):
        return remote(zsum.at[0, 0:HPAD], zh_in.at[n, slot], zh_s.at[0, 0], zh_r.at[n, slot], sibling)

    def stage_core(k):
        core_copy(k).wait_recv()
        parts[k, c] += core_in[k]
        zl_copy(k).start()

    def stage_zl(k):
        zl_copy(k).wait_recv()
        zsum[k] = parts[k, c, pl.ds(pl.multiple_of(zl * PAD, PAD), PAD)] + zl_in[k]
        for h in (0, 1):
            pl.when(zh != (k % 2) * 2 + h)(lambda h=h: zh_copy(k, h).start())

    def fin_refs(n, zi):
        return done.at[n, :, zi * 128 : zi * 128 + 256], fin_in.at[x]

    def fin_copy(n, zi):
        src, dst = fin_refs(n, zi)
        to = device(final_x[n], final_y[n], final_zh[n], zi, zh % 2)
        return remote(src, dst, fin_s.at[n, zi], fin_r.at[x], to)

    def stage_zh(n):
        for slot in range(3):
            zh_recv(n, slot).wait_recv()
        rows = pl.ds(pl.multiple_of((zh % 2) * HPAD, HPAD), HPAD)
        done[n] = zsum[2 * n + zh // 2, rows] + zh_in[n, 0] + zh_in[n, 1] + zh_in[n, 2]
        for zi in (0, 1):
            pl.when(is_self[n][zi])(lambda zi=zi: pltpu.make_async_copy(*fin_refs(n, zi), fin_r.at[x]).start())
            pl.when(jnp.logical_not(is_self[n][zi]))(lambda zi=zi: fin_copy(n, zi).start())

    def stage_fin():
        left = jnp.full((HROWS, HROWS), zl, jnp.int32) == 0
        for b in range(BLOCKS):
            remote(done.at[0, :, 0:256], fin_in.at[b], fin_s.at[0, 0], fin_r.at[b], sibling).wait_recv()
            v = fin_in[b, 0:HROWS] * (1.0 / 16384.0)
            for part in range(2):
                for h in range(2):
                    at = part * PAD + h * HPAD
                    gram_ref[part, :, b, h * HROWS : (h + 1) * HROWS] = jnp.where(
                        left, v[:, at : at + HROWS], v[:, 64 + at : 64 + at + HROWS]
                    )

    mine = pl.ds(pl.multiple_of(zl * HALF, HALF), HALF)
    theirs = pl.ds(pl.multiple_of(other * HALF, HALF), HALF)

    def put(b, lanes, rows):
        for at in range(BLOCKS):

            @pl.when(b == at)
            def _():
                for part in range(2):
                    basis_ref[part, :, at, lanes] = rows[part, 0:ROWS]

    def out_copy(o, t):
        to = device(mod(x + o, 4), y, zh, zl + t * (other - zl), c)
        return remote(bsend.at[o, t], bland.at[x, zl], out_s.at[o, t], out_r.at[x, zl], to)

    def out_recv(o, t):
        b, half = mod(x + o, 4), (zl, other)[t]
        return remote(bsend.at[o, t], bland.at[b, half], out_s.at[o, t], out_r.at[b, half], pooled(o, t))

    def basis(o):
        q = mod(x + o, 4)

        def rows_of(n, _):
            t = 1 - n
            prod = jnp.dot(ee[t].reshape(2 * PAD, KDIM), xs[q].reshape(KDIM, 2 * HALF), preferred_element_type=F32)
            bsend[o, t, 0] = (prod[:PAD, :HALF] - prod[PAD:, HALF:]).astype(jnp.bfloat16)
            bsend[o, t, 1] = (prod[PAD:, :HALF] + prod[:PAD, HALF:]).astype(jnp.bfloat16)
            own = (o == 0) & (t == 0)

            @pl.when(own)
            def _():
                put(x, mine, bsend.at[0, 0])

            pl.when(jnp.logical_not(own))(lambda: out_copy(o, t).start())
            return 0

        lax.fori_loop(0, 2, rows_of, 0)

    def basis_land(o, t):
        out_recv(o, t).wait_recv()
        b, half = mod(x + o, 4), (zl, other)[t]
        put(b, (mine, theirs)[t], bland.at[b, half])

    for o in (0, 3, 1, 2):
        for t in (0, 1):
            if (o, t) != (0, 0):
                scat_recv(o, t).wait_recv()
                near(0, o, t).start()
                near(1, o, t).start()
    pack_eig()
    eig_copy().start()
    parts[...] = jnp.zeros(parts.shape, F32)

    def hop_one(i, _):
        o = jnp.where(i == 0, 0, jnp.where(i == 1, 3, i - 1))
        for way in (0, 1):
            near_recv(way, o, 0).wait_recv()
            near_recv(way, o, 1).wait_recv()
            ring(way, o, 2).start()
        gram_partial(0, o)
        return 0

    def hop_two(i, _):
        o = jnp.where(i == 0, 0, jnp.where(i == 1, 3, i - 1))
        for way in (0, 1):
            ring_recv(way, o, 2).wait_recv()
            ring(way, o, 3).start()
        gram_partial(1, o)

        @pl.when(i == 2)
        def _():
            pl.when(zh < 3)(lambda: pl.semaphore_wait(above, 3 - zh))
            stage_zl(0)
            stage_zl(1)
            pl.when(c == 0)(lambda: stage_zl(3))

        return 0

    def hop_three(i, _):
        o = jnp.where(i == 0, 0, jnp.where(i == 1, 3, i - 1))
        for way in (0, 1):
            ring_recv(way, o, 3).wait_recv()
            pl.when(i >= 2)(lambda way=way: ring(way, 3 - 2 * (i - 2), 4).start())

        @pl.when(i == 0)
        def _():
            eig_copy().wait_recv()
            eig_forward().start()

        pl.when(i == ZL_SLOT)(lambda: stage_zl(2))
        pl.when(i == 3)(lambda: stage_zh(0))

        @pl.when(i == ZL_SLOT + 1)
        def _():
            pl.when(c == 1)(lambda: stage_zl(3))

        return 0

    def hop_four(i, _):
        o = jnp.where(i == 0, 3, jnp.where(i == 3, 0, i))
        for way in (0, 1):
            ring_recv(way, o, 4).wait_recv()
            pl.when(i < 2)(lambda way=way: ring(way, 2 - 2 * i, 4).start())
        basis(o)
        pl.when(i == ZH_SLOT)(lambda: stage_zh(1))
        return 0

    lax.fori_loop(0, 4, hop_one, 0)
    for k in (0, 1):
        core_copy(k).start()
    pl.when(c == 1)(lambda: core_copy(3).start())
    for k in (0, 1):
        stage_core(k)
    pl.when(c == 0)(lambda: stage_core(3))
    lax.fori_loop(0, 4, hop_two, 0)
    core_copy(2).start()
    pl.when(c == 0)(lambda: core_copy(3).start())
    stage_core(2)
    pl.when(c == 1)(lambda: stage_core(3))
    lax.fori_loop(0, 4, hop_three, 0)
    eig_forward_recv().wait_recv()
    lax.fori_loop(0, 4, hop_four, 0)
    for o in (1, 3, 2):
        for t in (0, 1):
            basis_land(o, t)
    stage_fin()
    basis_land(0, 1)

    for o, t in pool:
        scat_copy(o, t).wait_send()
        out_copy(o, t).wait_send()
    for way in (0, 1):
        for o in range(4):
            near(way, o, 0).wait_send()
            near(way, o, 1).wait_send()
            for d in (2, 3, 4):
                ring(way, o, d).wait_send()
    eig_copy().wait_send()
    eig_forward().wait_send()
    for k in range(4):
        core_copy(k).wait_send()
        zl_copy(k).wait_send()
        for h in (0, 1):
            pl.when(zh != (k % 2) * 2 + h)(lambda k=k, h=h: zh_copy(k, h).wait_send())
    for n in range(2):
        for zi in (0, 1):
            pl.when(jnp.logical_not(is_self[n][zi]))(lambda n=n, zi=zi: fin_copy(n, zi).wait_send())


def hand_on(basis_ref, gram_ref, basis_out, gram_out, basis_sem, gram_sem):
    copies = []
    for part in range(2):
        copies.append(pltpu.make_async_copy(basis_ref.at[part], basis_out.at[part], basis_sem.at[part]))
        copies.append(pltpu.make_async_copy(gram_ref.at[part], gram_out.at[part], gram_sem.at[part]))
    for copy in copies:
        copy.start()
    for copy in copies:
        copy.wait()


def local(responses, eigvecs):
    dma = pltpu.SemaphoreType.DMA
    bf, vm = jnp.bfloat16, pltpu.VMEM
    basis, gram = pl.pallas_call(
        kernel,
        out_shape=(
            jax.ShapeDtypeStruct((2, ROWS, BLOCKS, 2 * HALF), bf),
            jax.ShapeDtypeStruct((2, 45, BLOCKS, ROWS), F32),
        ),
        in_specs=[pl.BlockSpec(memory_space=pl.ANY)] * 2,
        out_specs=(pl.BlockSpec(memory_space=vm),) * 2,
        scratch_shapes=[
            vm((2, ROWS, BLOCKS, 2 * HALF), bf),
            vm((4, 2, RING, PAD, 2 * HALF), bf),
            vm((4, 2, PAD, 2 * HALF), bf),
            vm((2, ROWS, KDIM), bf),
            vm((2, 2, PAD, KDIM), bf),
            vm((4, 2, 2, PAD, HALF), bf),
            vm((4, 2, 2, PAD, HALF), bf),
            vm((4, 2, 2 * PAD, 4 * PAD), F32),
            vm((4, 2 * PAD, 4 * PAD), F32),
            vm((4, PAD, 4 * PAD), F32),
            vm((4, PAD, 4 * PAD), F32),
            vm((2, 3, HPAD, 4 * PAD), F32),
            vm((2, HPAD, 4 * PAD), F32),
            vm((BLOCKS, HPAD, 256), F32),
            dma((2,)), dma((4, 2)), dma((4, 2)), dma((2, 4, 2)), dma((2, 4, 2)), dma((2, 4, 3)), dma((2, 4, 3)),
            dma((2,)), dma, dma, dma, dma, dma((4, 2)), dma((4, 2)),
            dma((4,)), dma((4,)), dma((4,)), dma((4,)),
            dma((4, 2)), dma((2, 3)), dma((2, 2)), dma((4,)),
            pltpu.SemaphoreType.REGULAR,
        ],
        compiler_params=pltpu.CompilerParams(
            collective_id=0, has_side_effects=True, vmem_limit_bytes=60 * 2**20
        ),
    )(jnp.transpose(responses, (0, 2, 1, 3)), eigvecs)
    basis, gram = pl.pallas_call(
        hand_on,
        out_shape=(jax.ShapeDtypeStruct(basis.shape, bf), jax.ShapeDtypeStruct(gram.shape, F32)),
        in_specs=[pl.BlockSpec(memory_space=vm)] * 2,
        out_specs=(pl.BlockSpec(memory_space=pl.ANY),) * 2,
        scratch_shapes=[dma((2,)), dma((2,))],
    )(basis, gram)
    return jnp.transpose(gram, (0, 2, 3, 1)), jnp.transpose(basis, (0, 2, 1, 3))


def solution(mesh):
    specs = P(None, None, "exc", "unk")
    return jax.shard_map(local, mesh=mesh, in_specs=(specs, P("exc", None)), out_specs=(specs, specs), check_vma=False)
```

```python
import jax
import jax.numpy as jnp
from jax import lax
from jax.experimental import pallas as pl
from jax.experimental.pallas import tpu as pltpu
from jax.sharding import PartitionSpec as P

MESH = pl.DeviceIdType.MESH
ROWS, PAD, HALF = 90, 96, 256
BLOCKS, RING, GROUPS = 4, 8, 16
WAVES = ROWS * GROUPS
KDIM = PAD * GROUPS
ZL_SLOT, ZH_SLOT = 0, 1
HROWS, HPAD = 45, 48
F32 = jnp.float32


def mod(value, size):
    return lax.rem(value + 2 * size, size)


def device(x, y, zh, zl, c):
    return {"exc": zl * 8 + y, "unk": (zh * 4 + x) * 2 + c}


def row_of(k):
    return k - 4 * (k // 3)


def col_of(k, s):
    plus = jnp.where((k == 0) | (k == 3), 1, 0)
    return plus * (k // 3 + s) - (1 - plus) * (k // 2 + s)


def kernel(
    x_hbm, e_ref, basis_ref, gram_ref,
    x_ref, xs, staged, window, ee, bsend, bland, parts, core_in, zl_in, zsum, zh_in, done, fin_in,
    x_sem, scat_s, scat_r, near_s, near_r, ring_s, ring_r, win_s, eig_s, eig_r, fwd_s, fwd_r, out_s, out_r,
    core_s, core_r, zl_s, zl_r, zh_s, zh_r, fin_s, fin_r, above,
):
    exc, unk = lax.axis_index("exc"), lax.axis_index("unk")
    zl, y = exc // 8, exc % 8
    zh, x, c = unk // 8, (unk // 2) % 4, unk % 2
    other = 1 - zl
    up, down = device(x, mod(y + 1, 8), zh, zl, c), device(x, mod(y - 1, 8), zh, zl, c)
    pair = device(x, y, zh, other, c)
    sibling = device(x, y, zh, zl, 1 - c)
    pool = [(o, t) for o in (0, 1, 3, 2) for t in (1, 0) if (o, t) != (0, 0)]

    def pooled(o, t):
        return device(mod(x + o, 4), y, zh, (zl, other)[t], c)

    final_x, final_y, final_zh, is_self = [], [], [], []
    for n in range(2):
        k = 2 * n + zh // 2
        jy, iy = mod(y + row_of(k), 8), mod(y + col_of(k, c), 8)
        final_x.append(jy % 4)
        final_y.append(iy)
        final_zh.append(zl * 2 + jy // 4)
        here = (final_x[n] == x) & (iy == y) & (final_zh[n] == zh) & (zh % 2 == c)
        is_self.append([here & (zl == zi) for zi in (0, 1)])

    def remote(src, dst, send, recv, to):
        return pltpu.make_async_remote_copy(
            src_ref=src, dst_ref=dst, send_sem=send, recv_sem=recv, device_id=to, device_id_type=MESH
        )

    def win_copy(part):
        first = pl.multiple_of((part * 4 + x) * 1408 + part * 128, 128)
        return pltpu.make_async_copy(e_ref.at[:, pl.ds(first, KDIM)], window.at[part], win_s.at[part])

    x_copies = [pltpu.make_async_copy(x_hbm.at[part], x_ref.at[part], x_sem.at[part]) for part in range(2)]
    for copy in x_copies:
        copy.start()
    win_copy(0).start()
    win_copy(1).start()

    barrier = pltpu.get_barrier_semaphore()

    def greet(to):
        pl.semaphore_signal(barrier, inc=1, device_id=to, device_id_type=MESH)

    around = [up, down, sibling] + [pooled(o, t) for o, t in pool]
    for to in around:
        greet(to)
    for k in (1, 2, 3):
        pl.when(zh < k)(lambda k=k: greet(device(x, y, k, zl, c)))

    def scat_copy(o, t):
        return remote(staged.at[mod(x + o, 4), t], xs.at[x, zl, y], scat_s.at[o, t], scat_r.at[x, zl], pooled(o, t))

    def scat_recv(o, t):
        q, z = mod(x + o, 4), (zl, other)[t]
        return remote(staged.at[q, t], xs.at[q, z, y], scat_s.at[o, t], scat_r.at[q, z], pooled(o, t))

    def near(way, o, t):
        q, z = mod(x + o, 4), (zl, other)[t]
        ref = xs.at[q, z, y]
        return remote(ref, ref, near_s.at[way, o, t], near_r.at[way, q, z], (up, down)[way])

    def near_recv(way, o, z):
        q = mod(x + o, 4)
        ref = xs.at[q, z, mod(y - 1, 8) if way == 0 else mod(y + 1, 8)]
        return remote(ref, ref, near_s.at[way, o, z], near_r.at[way, q, z], (up, down)[way])

    def ring_ref(way, o, d, hop):
        src = mod(y - hop, 8) if way == 0 else mod(y + hop, 8)
        q = mod(x + o, 4)
        return xs.at[q, :, src] if d < 4 else xs.at[q, way, src]

    def ring(way, o, d):
        ref = ring_ref(way, o, d, d - 1)
        return remote(ref, ref, ring_s.at[way, o, d - 2], ring_r.at[way, o, d - 2], (up, down)[way])

    def ring_recv(way, o, d):
        ref = ring_ref(way, o, d, d)
        return remote(ref, ref, ring_s.at[way, o, d - 2], ring_r.at[way, o, d - 2], (up, down)[way])

    staged[...] = jnp.zeros(staged.shape, jnp.bfloat16)
    for copy in x_copies:
        copy.wait()
    for b in range(BLOCKS):
        for h in range(2):
            p, q = [x_ref[part, h * HROWS : (h + 1) * HROWS, b, :] for part in range(2)]
            low = jnp.concatenate([p[:, :HALF], q[:, :HALF]], axis=1)
            high = jnp.concatenate([p[:, HALF:], q[:, HALF:]], axis=1)
            first = jnp.full(low.shape, zl, jnp.int32) == 0
            staged[b, 0, h * HPAD : h * HPAD + HROWS, :] = jnp.where(first, low, high)
            staged[b, 1, h * HPAD : h * HPAD + HROWS, :] = jnp.where(first, high, low)
    xs[x, zl, y] = staged[x, 0]

    pl.semaphore_wait(barrier, len(around) + zh)
    for k in (0, 1, 2):

        @pl.when(zh > k)
        def _():
            pl.semaphore_signal(above, inc=1, device_id=device(x, y, k, zl, c), device_id_type=MESH)

    scat_copy(0, 1).start()
    near(0, 0, 0).start()
    near(1, 0, 0).start()
    for o, t in pool[1:]:
        scat_copy(o, t).start()

    def pack_eig():
        win_copy(0).wait()
        win_copy(1).wait()
        for part in range(2):
            ee[0, part] = jnp.zeros((PAD, KDIM), jnp.bfloat16)
        for at in range(4):

            @pl.when(x == at)
            def _():
                for part in range(2):
                    for i in range(2 * GROUPS):
                        first = at * 32 + i * HROWS
                        ee[0, part, 0:ROWS, i * HPAD : i * HPAD + HROWS] = window[part, :, first : first + HROWS]

    def eig_copy():
        return remote(ee.at[0, c], ee.at[1, c], eig_s, eig_r, pair)

    def eig_forward():
        return remote(ee.at[1, c], ee.at[1, c], fwd_s, fwd_r, sibling)

    def eig_forward_recv():
        return remote(ee.at[1, 1 - c], ee.at[1, 1 - c], fwd_s, fwd_r, sibling)

    def gram_partial(n, o):
        q = mod(x + o, 4)

        def one(t, _):
            k, s = (t // 2 + t // 4, t % 2) if n == 0 else (2 + t // 2, t % 2 + t // 2)
            rows = xs[q, :, mod(y + row_of(k), 8)].reshape(2 * PAD, 2 * HALF)
            cols = []
            for zi in range(2):
                v = xs[q, zi, mod(y + col_of(k, s), 8)]
                cols += [v, jnp.concatenate([-v[:, HALF:], v[:, :HALF]], axis=1)]
            right = jnp.concatenate(cols, axis=0)
            parts[k, s] += lax.dot_general(rows, right, (((1,), (1,)), ((), ())), preferred_element_type=F32)
            return 0

        lax.fori_loop(0, 5 - 2 * n, one, 0)

    def core_copy(k):
        return remote(parts.at[k, 1 - c], core_in.at[k], core_s.at[k], core_r.at[k], sibling)

    def zl_copy(k):
        rows = pl.ds(pl.multiple_of(other * PAD, PAD), PAD)
        return remote(parts.at[k, c, rows], zl_in.at[k], zl_s.at[k], zl_r.at[k], pair)

    def zh_copy(k, h):
        to = (k % 2) * 2 + h
        slot = mod(zh - to, 4) - 1
        return remote(
            zsum.at[k, h * HPAD : (h + 1) * HPAD], zh_in.at[k // 2, slot],
            zh_s.at[k, h], zh_r.at[k // 2, slot], device(x, y, to, zl, c),
        )

    def zh_recv(n, slot):
        return remote(zsum.at[0, 0:HPAD], zh_in.at[n, slot], zh_s.at[0, 0], zh_r.at[n, slot], sibling)

    def stage_core(k):
        core_copy(k).wait_recv()
        parts[k, c] += core_in[k]
        zl_copy(k).start()

    def stage_zl(k):
        zl_copy(k).wait_recv()
        zsum[k] = parts[k, c, pl.ds(pl.multiple_of(zl * PAD, PAD), PAD)] + zl_in[k]
        for h in (0, 1):
            pl.when(zh != (k % 2) * 2 + h)(lambda h=h: zh_copy(k, h).start())

    def fin_refs(n, zi):
        return done.at[n, :, zi * 128 : zi * 128 + 256], fin_in.at[x]

    def fin_copy(n, zi):
        src, dst = fin_refs(n, zi)
        to = device(final_x[n], final_y[n], final_zh[n], zi, zh % 2)
        return remote(src, dst, fin_s.at[n, zi], fin_r.at[x], to)

    def stage_zh(n):
        for slot in range(3):
            zh_recv(n, slot).wait_recv()
        rows = pl.ds(pl.multiple_of((zh % 2) * HPAD, HPAD), HPAD)
        done[n] = zsum[2 * n + zh // 2, rows] + zh_in[n, 0] + zh_in[n, 1] + zh_in[n, 2]
        for zi in (0, 1):
            pl.when(is_self[n][zi])(lambda zi=zi: pltpu.make_async_copy(*fin_refs(n, zi), fin_r.at[x]).start())
            pl.when(jnp.logical_not(is_self[n][zi]))(lambda zi=zi: fin_copy(n, zi).start())

    def stage_fin():
        left = jnp.full((HROWS, HROWS), zl, jnp.int32) == 0
        for b in range(BLOCKS):
            remote(done.at[0, :, 0:256], fin_in.at[b], fin_s.at[0, 0], fin_r.at[b], sibling).wait_recv()
            v = fin_in[b, 0:HROWS] * (1.0 / 16384.0)
            for part in range(2):
                for h in range(2):
                    at = part * PAD + h * HPAD
                    gram_ref[part, :, b, h * HROWS : (h + 1) * HROWS] = jnp.where(
                        left, v[:, at : at + HROWS], v[:, 64 + at : 64 + at + HROWS]
                    )

    mine = pl.ds(pl.multiple_of(zl * HALF, HALF), HALF)
    theirs = pl.ds(pl.multiple_of(other * HALF, HALF), HALF)

    def put(b, lanes, rows):
        for at in range(BLOCKS):

            @pl.when(b == at)
            def _():
                for part in range(2):
                    basis_ref[part, :, at, lanes] = rows[part, 0:ROWS]

    def out_copy(o, t):
        to = device(mod(x + o, 4), y, zh, zl + t * (other - zl), c)
        return remote(bsend.at[o, t], bland.at[x, zl], out_s.at[o, t], out_r.at[x, zl], to)

    def out_recv(o, t):
        b, half = mod(x + o, 4), (zl, other)[t]
        return remote(bsend.at[o, t], bland.at[b, half], out_s.at[o, t], out_r.at[b, half], pooled(o, t))

    def basis(o):
        q = mod(x + o, 4)

        def rows_of(n, _):
            t = 1 - n
            prod = jnp.dot(ee[t].reshape(2 * PAD, KDIM), xs[q].reshape(KDIM, 2 * HALF), preferred_element_type=F32)
            bsend[o, t, 0] = (prod[:PAD, :HALF] - prod[PAD:, HALF:]).astype(jnp.bfloat16)
            bsend[o, t, 1] = (prod[PAD:, :HALF] + prod[:PAD, HALF:]).astype(jnp.bfloat16)
            own = (o == 0) & (t == 0)

            @pl.when(own)
            def _():
                put(x, mine, bsend.at[0, 0])

            pl.when(jnp.logical_not(own))(lambda: out_copy(o, t).start())
            return 0

        lax.fori_loop(0, 2, rows_of, 0)

    def basis_land(o, t):
        out_recv(o, t).wait_recv()
        b, half = mod(x + o, 4), (zl, other)[t]
        put(b, (mine, theirs)[t], bland.at[b, half])

    for o in (0, 3, 1, 2):
        for t in (0, 1):
            if (o, t) != (0, 0):
                scat_recv(o, t).wait_recv()
                near(0, o, t).start()
                near(1, o, t).start()
    pack_eig()
    eig_copy().start()
    parts[...] = jnp.zeros(parts.shape, F32)

    def hop_one(i, _):
        o = jnp.where(i == 0, 0, jnp.where(i == 1, 3, i - 1))
        for way in (0, 1):
            near_recv(way, o, 0).wait_recv()
            near_recv(way, o, 1).wait_recv()
            ring(way, o, 2).start()
        gram_partial(0, o)
        return 0

    def hop_two(i, _):
        o = jnp.where(i == 0, 0, jnp.where(i == 1, 3, i - 1))
        for way in (0, 1):
            ring_recv(way, o, 2).wait_recv()
            ring(way, o, 3).start()
        gram_partial(1, o)

        @pl.when(i == 2)
        def _():
            pl.when(zh < 3)(lambda: pl.semaphore_wait(above, 3 - zh))
            stage_zl(0)
            stage_zl(1)
            pl.when(c == 0)(lambda: stage_zl(3))

        return 0

    def hop_three(i, _):
        o = jnp.where(i == 0, 0, jnp.where(i == 1, 3, i - 1))
        for way in (0, 1):
            ring_recv(way, o, 3).wait_recv()
            ring(way, o, 4).start()

        @pl.when(i == 0)
        def _():
            eig_copy().wait_recv()
            eig_forward().start()

        pl.when(i == ZL_SLOT)(lambda: stage_zl(2))
        pl.when(i == 3)(lambda: stage_zh(0))

        @pl.when(i == ZL_SLOT + 1)
        def _():
            pl.when(c == 1)(lambda: stage_zl(3))

        return 0

    def hop_four(i, _):
        o = jnp.where(i == 0, 3, jnp.where(i == 3, 0, i))
        for way in (0, 1):
            ring_recv(way, o, 4).wait_recv()
        basis(o)
        pl.when(i == ZH_SLOT)(lambda: stage_zh(1))
        return 0

    lax.fori_loop(0, 4, hop_one, 0)
    for k in (0, 1):
        core_copy(k).start()
    pl.when(c == 1)(lambda: core_copy(3).start())
    for k in (0, 1):
        stage_core(k)
    pl.when(c == 0)(lambda: stage_core(3))
    lax.fori_loop(0, 4, hop_two, 0)
    core_copy(2).start()
    pl.when(c == 0)(lambda: core_copy(3).start())
    stage_core(2)
    pl.when(c == 1)(lambda: stage_core(3))
    lax.fori_loop(0, 4, hop_three, 0)
    eig_forward_recv().wait_recv()
    lax.fori_loop(0, 4, hop_four, 0)
    for o in (1, 3, 2):
        for t in (0, 1):
            basis_land(o, t)
    stage_fin()
    basis_land(0, 1)

    for o, t in pool:
        scat_copy(o, t).wait_send()
        out_copy(o, t).wait_send()
    for way in (0, 1):
        for o in range(4):
            near(way, o, 0).wait_send()
            near(way, o, 1).wait_send()
            for d in (2, 3, 4):
                ring(way, o, d).wait_send()
    eig_copy().wait_send()
    eig_forward().wait_send()
    for k in range(4):
        core_copy(k).wait_send()
        zl_copy(k).wait_send()
        for h in (0, 1):
            pl.when(zh != (k % 2) * 2 + h)(lambda k=k, h=h: zh_copy(k, h).wait_send())
    for n in range(2):
        for zi in (0, 1):
            pl.when(jnp.logical_not(is_self[n][zi]))(lambda n=n, zi=zi: fin_copy(n, zi).wait_send())


def hand_on(basis_ref, gram_ref, basis_out, gram_out, basis_sem, gram_sem):
    copies = []
    for part in range(2):
        copies.append(pltpu.make_async_copy(basis_ref.at[part], basis_out.at[part], basis_sem.at[part]))
        copies.append(pltpu.make_async_copy(gram_ref.at[part], gram_out.at[part], gram_sem.at[part]))
    for copy in copies:
        copy.start()
    for copy in copies:
        copy.wait()


def local(responses, eigvecs):
    dma = pltpu.SemaphoreType.DMA
    bf, vm = jnp.bfloat16, pltpu.VMEM
    basis, gram = pl.pallas_call(
        kernel,
        out_shape=(
            jax.ShapeDtypeStruct((2, ROWS, BLOCKS, 2 * HALF), bf),
            jax.ShapeDtypeStruct((2, 45, BLOCKS, ROWS), F32),
        ),
        in_specs=[pl.BlockSpec(memory_space=pl.ANY)] * 2,
        out_specs=(pl.BlockSpec(memory_space=vm),) * 2,
        scratch_shapes=[
            vm((2, ROWS, BLOCKS, 2 * HALF), bf),
            vm((4, 2, RING, PAD, 2 * HALF), bf),
            vm((4, 2, PAD, 2 * HALF), bf),
            vm((2, ROWS, KDIM), bf),
            vm((2, 2, PAD, KDIM), bf),
            vm((4, 2, 2, PAD, HALF), bf),
            vm((4, 2, 2, PAD, HALF), bf),
            vm((4, 2, 2 * PAD, 4 * PAD), F32),
            vm((4, 2 * PAD, 4 * PAD), F32),
            vm((4, PAD, 4 * PAD), F32),
            vm((4, PAD, 4 * PAD), F32),
            vm((2, 3, HPAD, 4 * PAD), F32),
            vm((2, HPAD, 4 * PAD), F32),
            vm((BLOCKS, HPAD, 256), F32),
            dma((2,)), dma((4, 2)), dma((4, 2)), dma((2, 4, 2)), dma((2, 4, 2)), dma((2, 4, 3)), dma((2, 4, 3)),
            dma((2,)), dma, dma, dma, dma, dma((4, 2)), dma((4, 2)),
            dma((4,)), dma((4,)), dma((4,)), dma((4,)),
            dma((4, 2)), dma((2, 3)), dma((2, 2)), dma((4,)),
            pltpu.SemaphoreType.REGULAR,
        ],
        compiler_params=pltpu.CompilerParams(
            collective_id=0, has_side_effects=True, vmem_limit_bytes=60 * 2**20
        ),
    )(jnp.transpose(responses, (0, 2, 1, 3)), eigvecs)
    basis, gram = pl.pallas_call(
        hand_on,
        out_shape=(jax.ShapeDtypeStruct(basis.shape, bf), jax.ShapeDtypeStruct(gram.shape, F32)),
        in_specs=[pl.BlockSpec(memory_space=vm)] * 2,
        out_specs=(pl.BlockSpec(memory_space=pl.ANY),) * 2,
        scratch_shapes=[dma((2,)), dma((2,))],
    )(basis, gram)
    return jnp.transpose(gram, (0, 2, 3, 1)), jnp.transpose(basis, (0, 2, 1, 3))


def solution(mesh):
    specs = P(None, None, "exc", "unk")
    return jax.shard_map(local, mesh=mesh, in_specs=(specs, P("exc", None)), out_specs=(specs, specs), check_vma=False)
```
